32 devices in a mesh: tile: 16 (over z, x, core), loop: 2 (over y).
Axes of the slice: x: 2, y: 2, z: 4, core: 2. Of those that a mesh axis runs over, the one named last changes fastest.
Arguments:
- star_slot: int32 [16, 32, 128], P('tile', 'loop'), may hold values from 0 to 255
- star_block: int32 [16, 32], P('tile', 'loop'), may hold values from 0 to 1, as said below
- exposure: int32 [16, 32, 128], P('tile', 'loop'), may hold values from 0 to 511
- superpixel: int32 [16, 32, 128], P('tile', 'loop'), may hold values from 0 to 2047
- magnitude: float32 [16, 32, 128], P('tile', 'loop'), may hold values from -7 to 7
- weight: float32 [16, 32, 128], P('tile', 'loop'), may hold values from 0.25 to 4
Outputs:
- star_mags: float32 [16384], P(('tile', 'loop'))
- zero_points: float32 [1024], P('loop')
- flat_field: float32 [128, 256], P('tile')
The draws below stay inside these ranges and needn't reach their ends.
Inputs may be any that keep to these rules, and one draw needn't show every extreme that they name: `star_block`: observation blocks of one device at positions 8 * o to 8 * o + 7 of its 16 blocks observe stars of the star shard held by loop index o of the same tile.
All inputs are finite; a program needn't handle non-finite values.
Results may differ from the reference program's by a relative error of at most 0.00022.
Values sent between devices are 32-bit elements; how exact they have to be, the bound alone decides.
A program may use at most 64 MiB of HBM per device.

```python
import math
import jax
import jax.numpy as jnp
from jax import lax

FC = 256
ROWS_DEV = 8
BLK_DEV = 16
SBLK_DEV = 2
EXP_DEV = 512
STAR_BLK = 256
OBS_BLK = 128
ITERS = 2
TILES = 16
GROUPS = 2
BLK_OWN = 8
STAR_DEV = 512
STARS = 16384
EXPOSURES = 1024
FLAT_ROWS = 128
OBS_ROWS = 32


def observation_tables(key):
    tile_count = FLAT_ROWS // ROWS_DEV
    group_count = EXPOSURES // EXP_DEV
    row_count = BLK_DEV * group_count
    keys = jax.random.split(jax.random.fold_in(key, 101), 4)
    slots = jax.random.randint(keys[0], (tile_count, row_count, OBS_BLK), 0, STAR_BLK, dtype=jnp.int32)
    blocks = jax.random.randint(keys[1], (tile_count, row_count), 0, SBLK_DEV, dtype=jnp.int32)
    exposures = jax.random.randint(keys[2], (tile_count, row_count, OBS_BLK), 0, EXP_DEV, dtype=jnp.int32)
    pixels = jax.random.randint(keys[3], (tile_count, row_count, OBS_BLK), 0, ROWS_DEV * FC, dtype=jnp.int32)
    return (slots, blocks, exposures, pixels)


def draw_star_slot(key, part):
    return observation_tables(key)[0]


def draw_star_block(key, part):
    return observation_tables(key)[1]


def draw_exposure(key, part):
    return observation_tables(key)[2]


def draw_superpixel(key, part):
    return observation_tables(key)[3]


def draw_magnitude(key, part):
    slots, blocks, exposures, pixels = observation_tables(key)
    group_count = EXPOSURES // EXP_DEV
    tile_ids = lax.broadcasted_iota(jnp.int32, slots.shape, 0)
    row_ids = lax.broadcasted_iota(jnp.int32, slots.shape, 1)
    group_ids = row_ids // BLK_DEV
    owner_ids = row_ids % BLK_DEV // (BLK_DEV // group_count)
    star_ids = (tile_ids * group_count + owner_ids) * STAR_DEV + blocks[:, :, None] * STAR_BLK + slots
    expo_ids = group_ids * EXP_DEV + exposures
    pixel_ids = tile_ids * (ROWS_DEV * FC) + pixels
    keys = jax.random.split(jax.random.fold_in(key, 202), 4)
    star_true = jnp.clip(jax.random.normal(keys[0], (STARS,), jnp.float32), -4.0, 4.0)
    expo_true = jnp.clip(0.4 * jax.random.normal(keys[1], (EXPOSURES,), jnp.float32), -1.6, 1.6)
    flat_true = jnp.clip(0.25 * jax.random.normal(keys[2], (FLAT_ROWS * FC,), jnp.float32), -1.0, 1.0)
    noise = jnp.clip(0.1 * jax.random.normal(keys[3], slots.shape, jnp.float32), -0.4, 0.4)
    values = star_true[star_ids] + expo_true[expo_ids] + flat_true[pixel_ids] + noise
    return values.astype(jnp.float32)


def steps_of(stream_key, dims, pieces, smallest, largest):
    gain = 1.0
    for axis_at, parts in pieces:
        draws = jax.random.uniform(jax.random.fold_in(jax.random.fold_in(stream_key, 6), axis_at), (parts,), jnp.float32, smallest / len(pieces), largest / len(pieces))
        gain = gain * jnp.repeat(jnp.exp(draws), dims[axis_at] // parts).reshape((-1,) + (1,) * (len(dims) - 1 - axis_at))
    return gain


def setup_inputs(seed: int = 0) -> dict:
    seeds = jax.random.split(jax.random.key(seed), 7)
    return {
        "star_slot": draw_star_slot(jax.random.fold_in(seeds[6], 71), 0),
        "star_block": draw_star_block(jax.random.fold_in(seeds[6], 71), 0),
        "exposure": draw_exposure(jax.random.fold_in(seeds[6], 71), 0),
        "superpixel": draw_superpixel(jax.random.fold_in(seeds[6], 71), 0),
        "magnitude": draw_magnitude(jax.random.fold_in(seeds[6], 71), 0),
        "weight": jnp.clip(jnp.exp(math.log(4.0) - 2.7725887 * jax.random.uniform(seeds[5], (TILES, OBS_ROWS, OBS_BLK), jnp.float32) ** steps_of(seeds[5], (TILES, OBS_ROWS, OBS_BLK), ((0, 16), (1, 2)), -0.2, 0.2)), 0.25, 4.0),
    }


SMOOTH = 2.0
RIDGE = 0.5


def observation_indices(star_slot, star_block, exposure, superpixel):
    tile_ids = lax.broadcasted_iota(jnp.int32, star_slot.shape, 0)
    row_ids = lax.broadcasted_iota(jnp.int32, star_slot.shape, 1)
    group_ids = row_ids // BLK_DEV
    owner_ids = (row_ids % BLK_DEV) // BLK_OWN
    star_ids = (tile_ids * GROUPS + owner_ids) * STAR_DEV + star_block[:, :, None] * STAR_BLK + star_slot
    expo_ids = group_ids * EXP_DEV + exposure
    pixel_ids = tile_ids * (ROWS_DEV * FC) + superpixel
    return star_ids.reshape(-1), expo_ids.reshape(-1), pixel_ids.reshape(-1)


def laplace(flat):
    padded = jnp.pad(flat, 1)
    beside = padded[2:, 1:-1] + padded[:-2, 1:-1] + padded[1:-1, 2:] + padded[1:-1, :-2]
    return SMOOTH * (4.0 * flat - beside)


def combine(vector, other, factor):
    return jax.tree.map(lambda values, others: values + factor * others, vector, other)


def reference(star_slot, star_block, exposure, superpixel, magnitude, weight):
    star_ids, expo_ids, pixel_ids = observation_indices(star_slot, star_block, exposure, superpixel)
    weights = weight.reshape(-1)
    magnitudes = magnitude.reshape(-1)
    pixels = FLAT_ROWS * FC

    def adjoint(values):
        return (jax.ops.segment_sum(values, star_ids, num_segments=STARS),
                jax.ops.segment_sum(values, expo_ids, num_segments=EXPOSURES),
                jax.ops.segment_sum(values, pixel_ids, num_segments=pixels).reshape(FLAT_ROWS, FC))

    right_side = adjoint(weights * magnitudes)
    counts = adjoint(weights)
    diagonal = (counts[0] + RIDGE, counts[1] + RIDGE, counts[2] + (4.0 * SMOOTH + RIDGE))

    def operate(vector):
        fitted = vector[0][star_ids] + vector[1][expo_ids] + vector[2].reshape(-1)[pixel_ids]
        sums = adjoint(weights * fitted)
        return (sums[0] + RIDGE * vector[0], sums[1] + RIDGE * vector[1],
                sums[2] + laplace(vector[2]) + RIDGE * vector[2])

    def inner(first_vec, second_vec):
        return (jnp.sum(first_vec[0] * second_vec[0]) + jnp.sum(first_vec[1] * second_vec[1])
                + jnp.sum(first_vec[2] * second_vec[2]))

    def divide(vector):
        return jax.tree.map(lambda values, scales: values / scales, vector, diagonal)

    solution = jax.tree.map(jnp.zeros_like, right_side)
    residual = right_side
    precon = divide(residual)
    norm_now = inner(residual, precon)
    direction = precon
    for iteration in range(ITERS):
        image = operate(direction)
        step_size = norm_now / inner(direction, image)
        solution = combine(solution, direction, step_size)
        residual = combine(residual, image, -step_size)
        if iteration + 1 < ITERS:
            precon = divide(residual)
            norm_next = inner(residual, precon)
            direction = combine(precon, direction, norm_next / norm_now)
            norm_now = norm_next
    return (solution[0], solution[1], solution[2])
```

```python
import functools

import jax
import jax.numpy as jnp
from jax import lax
from jax.experimental import pallas as pl
from jax.experimental.pallas import tpu as pltpu
from jax.sharding import PartitionSpec as P

FC = 256
ROWS_DEV = 8
SBLK_DEV = 2
EXP_DEV = 512
STAR_BLK = 256

SMOOTH = 2.0
RIDGE = 0.5

LANES = 128
HALVES = FC // LANES
STAR_ROWS = SBLK_DEV * STAR_BLK // LANES
EXPO_ROWS = EXP_DEV // LANES
FLAT_ROWS = HALVES * ROWS_DEV
MESH = pl.DeviceIdType.MESH
F32 = jnp.float32
BF16 = jnp.bfloat16


def pieces(values):
    high = values.astype(BF16)
    low = (values - high.astype(F32)).astype(BF16)
    return high, low


def fold(items):
    total = items[0]
    for item in items[1:]:
        total = total + item
    return total


def lane_fold(row):
    row = jnp.sum(row, axis=0, keepdims=True)
    return fold([row[:, at : at + LANES] for at in range(0, row.shape[1], LANES)])


def line(rows):
    return jnp.concatenate([rows[b : b + 1, :] for b in range(rows.shape[0])], axis=1)


def beside_columns(flat):
    column = lax.broadcasted_iota(jnp.int32, flat.shape, 1)
    left = jnp.where(column == 0, 0.0, pltpu.roll(flat, 1, 1))
    right = jnp.where(column == FC - 1, 0.0, pltpu.roll(flat, FC - 1, 1))
    return left + right


def kernel(
    tiles, loops,
    slot_ref, block_ref, expo_ref, pixel_ref, mag_ref, weight_ref,
    star_out, expo_out, flat_out,
    hot, mask, edges0, edges1, ext,
    loop0, loop1, expo0, expo1, halo0, halo1, dots0, dots1,
    send, recv,
):
    tile = lax.axis_index("tile")
    loop = lax.axis_index("loop")
    everyone = tiles * loops
    rank = tile * loops + loop
    blocks = slot_ref.shape[1]
    per_shard = blocks // loops
    star_rows = loops * STAR_ROWS
    expo_at = star_rows
    flat_at = star_rows + 8
    rows = flat_at + FLAT_ROWS

    def other(d):
        peer = lax.rem(rank + d, everyone)
        return peer // loops, lax.rem(peer, loops)

    barrier = pltpu.get_barrier_semaphore()

    def greet(d, carry):
        pl.semaphore_signal(barrier, inc=1, device_id=other(d), device_id_type=MESH)
        return carry

    lax.fori_loop(1, everyone, greet, 0)

    def push(src, dst, which, device):
        pltpu.make_async_remote_copy(
            src_ref=src, dst_ref=dst, send_sem=send.at[which], recv_sem=recv.at[which],
            device_id=device, device_id_type=MESH,
        ).start()

    def settle(buffer, count, sem):
        part = buffer.at[pl.ds(0, count)]
        pltpu.make_async_copy(part, part, sem).wait()

    def push_tiles(buffer, which):
        def step(d, carry):
            push(buffer.at[tile], buffer.at[tile], which, (lax.rem(tile + d, tiles), loop))
            return carry

        lax.fori_loop(1, tiles, step, 0)

    def push_loops(buffer, which):
        for d in range(1, loops):
            push(buffer.at[loop], buffer.at[loop], which, (tile, lax.rem(loop + d, loops)))

    def push_edges(edges, buffer, which):
        above = lax.rem(tile + tiles - 1, tiles)
        below = lax.rem(tile + 1, tiles)
        for d in range(loops):
            to = lax.rem(loop + d, loops)
            push(edges, buffer.at[loops + loop], which, (above, to))
            push(edges, buffer.at[loop], which, (below, to))

    def push_dots(buffer, which):
        def step(d, carry):
            push(buffer.at[rank], buffer.at[rank], which, other(d))
            return carry

        lax.fori_loop(1, everyone, step, 0)

    lane_ids = lax.broadcasted_iota(jnp.int32, (LANES, LANES), 0)
    star_ids = lax.broadcasted_iota(jnp.int32, (star_rows, LANES), 0)
    expo_ids = lax.broadcasted_iota(jnp.int32, (8, LANES), 0)
    flat_ids = lax.broadcasted_iota(jnp.int32, (FLAT_ROWS, LANES), 0)
    for b in range(blocks):
        at = slice(b * LANES, (b + 1) * LANES)
        star = block_ref[0, b] * STAR_BLK + slot_ref[0, b : b + 1, :]
        expo = expo_ref[0, b : b + 1, :]
        pixel = pixel_ref[0, b : b + 1, :]
        for k, ids in enumerate((star, expo, pixel)):
            hot[k * LANES : (k + 1) * LANES, at] = jnp.where(
                lane_ids == (ids & (LANES - 1)), 1.0, 0.0
            ).astype(BF16)
        star_high = (b // per_shard) * STAR_ROWS + star // LANES
        pixel_high = (pixel // LANES) % HALVES * ROWS_DEV + pixel // FC
        mask[0:star_rows, at] = jnp.where(star_ids == star_high, 1.0, 0.0)
        mask[expo_at : expo_at + 8, at] = jnp.where(expo_ids == expo // LANES, 1.0, 0.0)
        mask[flat_at:rows, at] = jnp.where(flat_ids == pixel_high, 1.0, 0.0)

    weights = line(weight_ref[0])
    weighted = weights * line(mag_ref[0])

    def scatter(*values):
        parts = []
        for value in values:
            for piece in pieces(value):
                parts.append((mask[...] * piece.astype(F32)).astype(BF16))
        sums = lax.dot_general(
            jnp.concatenate(parts, axis=0), hot[...], (((1,), (1,)), ((), ())),
            preferred_element_type=F32,
        )
        out = []
        for k in range(len(values)):
            both = sums[2 * k * rows : (2 * k + 1) * rows] + sums[(2 * k + 1) * rows : (2 * k + 2) * rows]
            flat = both[flat_at:rows, 2 * LANES : 3 * LANES]
            flat = jnp.concatenate(
                [flat[h * ROWS_DEV : (h + 1) * ROWS_DEV] for h in range(HALVES)], axis=1
            )
            out.append((
                both[0:star_rows, 0:LANES],
                both[expo_at : expo_at + EXPO_ROWS, LANES : 2 * LANES],
                flat,
            ))
        return out

    def gather(star, expo, flat):
        flat = jnp.concatenate([flat[:, h * LANES : (h + 1) * LANES] for h in range(HALVES)], axis=0)
        expo = jnp.concatenate([expo, jnp.zeros((8 - EXPO_ROWS, LANES), F32)], axis=0)

        def place(part, k):
            return jnp.concatenate(
                [part if j == k else jnp.zeros_like(part) for j in range(3)], axis=1
            )

        values = jnp.concatenate([place(star, 0), place(expo, 1), place(flat, 2)], axis=0)
        found = jnp.dot(
            jnp.concatenate(pieces(values), axis=0), hot[...], preferred_element_type=F32
        )
        return jnp.sum((found[0:rows] + found[rows:]) * mask[...], axis=0, keepdims=True)

    (rhs, count) = scatter(weighted, weights)
    expo0[tile] = jnp.concatenate([rhs[1], count[1]], axis=0)
    loop0[loop] = jnp.concatenate(
        [rhs[0], count[0]]
        + [part[2][:, h * LANES : (h + 1) * LANES] for part in (rhs, count) for h in range(HALVES)],
        axis=0,
    )
    edges0[0:2] = rhs[2][0:2]
    edges0[2:4] = count[2][0:2]
    edges0[4:6] = rhs[2][ROWS_DEV - 2 :]
    edges0[6:8] = count[2][ROWS_DEV - 2 :]
    pl.semaphore_wait(barrier, everyone - 1)
    push_tiles(expo0, 0)
    push_edges(edges0, halo0, 2)
    push_loops(loop0, 1)

    settle(loop0, loops - 1, recv.at[1])
    joint = fold([loop0[l] for l in range(loops)])
    rhs_star = joint[0:star_rows]
    diag_star = joint[star_rows : 2 * star_rows] + RIDGE
    joint = joint[2 * star_rows :]
    rhs_mine, count_mine = [
        jnp.concatenate(
            [joint[(k * HALVES + h) * ROWS_DEV : (k * HALVES + h + 1) * ROWS_DEV] for h in range(HALVES)],
            axis=1,
        )
        for k in range(2)
    ]
    settle(halo0, 2 * loops, recv.at[2])
    over = fold([halo0[l] for l in range(loops)])
    under = fold([halo0[loops + l] for l in range(loops)])
    over = jnp.where(tile > 0, over, 0.0)
    under = jnp.where(tile < tiles - 1, under, 0.0)
    inner = slice(2, 2 + ROWS_DEV)
    wide = slice(1, 3 + ROWS_DEV)
    whole = slice(0, 4 + ROWS_DEV)
    ext[0, inner] = rhs_mine
    ext[0, 0:2] = over[4:6]
    ext[0, 2 + ROWS_DEV : 4 + ROWS_DEV] = under[0:2]
    ext[1, inner] = count_mine
    ext[1, 0:2] = over[6:8]
    ext[1, 2 + ROWS_DEV : 4 + ROWS_DEV] = under[2:4]
    ext[2, whole] = ext[0, whole] / (ext[1, whole] + (4.0 * SMOOTH + RIDGE))
    g_star = rhs_star / diag_star
    g_flat = ext[2, inner]
    settle(expo0, tiles - 1, recv.at[0])
    joint = fold([expo0[t] for t in range(tiles)])
    rhs_expo = joint[0:EXPO_ROWS]
    diag_expo = joint[EXPO_ROWS:] + RIDGE
    g_expo = rhs_expo / diag_expo

    shard_row = lax.broadcasted_iota(jnp.int32, (star_rows, LANES), 0) // STAR_ROWS
    own_star = jnp.where(shard_row == loop, 1.0, 0.0)
    own_expo = jnp.where(tile == 0, 1.0, 0.0)
    own_flat = jnp.where(loop == 0, 1.0, 0.0)

    def inner_rows(star, expo, flat):
        return (
            lane_fold(own_star * star) + own_expo * lane_fold(expo) + own_flat * lane_fold(flat)
        )

    fitted = gather(g_star, g_expo, g_flat)
    pulled = weights * fitted
    ((sum_star, sum_expo, sum_flat),) = scatter(pulled)
    expo1[tile, 0:EXPO_ROWS] = sum_expo
    loop1[loop] = jnp.concatenate(
        [sum_star] + [sum_flat[:, h * LANES : (h + 1) * LANES] for h in range(HALVES)], axis=0
    )
    edges1[0:1] = sum_flat[0:1]
    edges1[1:2] = sum_flat[ROWS_DEV - 1 :]
    push_tiles(expo1, 3)
    push_edges(edges1, halo1, 5)
    push_loops(loop1, 4)
    v = ext[2, wide]
    smooth = SMOOTH * (4.0 * v - ext[2, 0 : 2 + ROWS_DEV] - ext[2, 2 : 4 + ROWS_DEV] - beside_columns(v)) + RIDGE * v
    ext[3, wide] = smooth
    smooth_mine = ext[3, inner]
    dots0[rank, 0:1] = inner_rows(rhs_star * g_star, rhs_expo * g_expo, rhs_mine * g_flat)
    dots0[rank, 1:2] = lane_fold(pulled * fitted) + inner_rows(
        RIDGE * g_star * g_star, RIDGE * g_expo * g_expo, smooth_mine * g_flat
    )
    push_dots(dots0, 6)

    settle(loop1, loops - 1, recv.at[4])
    joint = fold([loop1[l] for l in range(loops)])
    image_star = joint[0:star_rows] + RIDGE * g_star
    sum_mine = jnp.concatenate(
        [joint[star_rows + h * ROWS_DEV : star_rows + (h + 1) * ROWS_DEV] for h in range(HALVES)], axis=1
    )
    settle(halo1, 2 * loops, recv.at[5])
    over = fold([halo1[l] for l in range(loops)])
    under = fold([halo1[loops + l] for l in range(loops)])
    ext[4, inner] = sum_mine
    ext[4, 1:2] = over[1:2]
    ext[4, 2 + ROWS_DEV : 3 + ROWS_DEV] = under[0:1]
    row = lax.broadcasted_iota(jnp.int32, (2 + ROWS_DEV, FC), 0)
    inside = ((row > 0) | (tile > 0)) & ((row < 1 + ROWS_DEV) | (tile < tiles - 1))
    image_wide = jnp.where(inside, ext[4, wide] + smooth, 0.0)
    settle(expo1, tiles - 1, recv.at[3])
    joint = fold([expo1[t, 0:EXPO_ROWS] for t in range(tiles)])
    image_expo = joint + RIDGE * g_expo

    def total(buffer, which, count):
        settle(buffer, everyone - 1, recv.at[which])
        joint = fold([buffer[r] for r in range(everyone)])
        return [jnp.sum(joint[k : k + 1], axis=1, keepdims=True) for k in range(count)]

    norm, curve = total(dots0, 6, 2)
    alpha = norm / curve

    res_star = rhs_star - alpha * image_star
    res_expo = rhs_expo - alpha * image_expo
    res_wide = ext[0, wide] - alpha * image_wide
    h_star = res_star / diag_star
    h_expo = res_expo / diag_expo
    ext[5, wide] = res_wide / (ext[1, wide] + (4.0 * SMOOTH + RIDGE))
    ext[6, wide] = res_wide
    ext[7, wide] = image_wide
    h_flat = ext[5, inner]
    fitted = gather(h_star, h_expo, h_flat)
    beside = ext[5, 1 : 1 + ROWS_DEV] + ext[5, 3 : 3 + ROWS_DEV] + beside_columns(h_flat)
    dots1[rank, 0:1] = inner_rows(res_star * h_star, res_expo * h_expo, ext[6, inner] * h_flat)
    dots1[rank, 1:2] = inner_rows(image_star * h_star, image_expo * h_expo, ext[7, inner] * h_flat)
    dots1[rank, 2:3] = lane_fold(weights * fitted * fitted) + inner_rows(
        RIDGE * h_star * h_star,
        RIDGE * h_expo * h_expo,
        (SMOOTH * (4.0 * h_flat - beside) + RIDGE * h_flat) * h_flat,
    )
    push_dots(dots1, 7)
    norm_next, cross, curve_next = total(dots1, 7, 3)
    ratio = norm_next / norm
    step = norm_next / (curve_next + ratio * (2.0 * cross + ratio * curve))

    def solve(first, second):
        return alpha * first + step * (second + ratio * first)

    star = solve(g_star, h_star)
    star_out[...] = fold([
        jnp.where(loop == l, star[l * STAR_ROWS : (l + 1) * STAR_ROWS], 0.0) for l in range(loops)
    ])
    expo_out[...] = solve(g_expo, h_expo)
    flat_out[...] = solve(g_flat, h_flat)

    for which, (buffer, count) in enumerate((
        (expo0, tiles - 1), (loop0, loops - 1), (halo0, 2 * loops),
        (expo1, tiles - 1), (loop1, loops - 1), (halo1, 2 * loops),
        (dots0, everyone - 1), (dots1, everyone - 1),
    )):
        settle(buffer, count, send.at[which])


def on_device(tiles, loops, star_slot, star_block, exposure, superpixel, magnitude, weight):
    blocks = star_slot.shape[1]
    seen = blocks * LANES
    star_rows = loops * STAR_ROWS
    rows = star_rows + 8 + FLAT_ROWS
    vmem = pl.BlockSpec(memory_space=pltpu.VMEM)
    star, expo, flat = pl.pallas_call(
        functools.partial(kernel, tiles, loops),
        out_shape=(
            jax.ShapeDtypeStruct((STAR_ROWS, LANES), F32),
            jax.ShapeDtypeStruct((EXPO_ROWS, LANES), F32),
            jax.ShapeDtypeStruct((ROWS_DEV, FC), F32),
        ),
        in_specs=[vmem, pl.BlockSpec(memory_space=pltpu.SMEM)] + [vmem] * 4,
        out_specs=(vmem, vmem, vmem),
        scratch_shapes=[
            pltpu.VMEM((3 * LANES, seen), BF16),
            pltpu.VMEM((rows, seen), F32),
            pltpu.VMEM((8, FC), F32),
            pltpu.VMEM((8, FC), F32),
            pltpu.VMEM((8, ROWS_DEV + 8, FC), F32),
            pltpu.VMEM((loops, 2 * (star_rows + FLAT_ROWS), LANES), F32),
            pltpu.VMEM((loops, star_rows + FLAT_ROWS, LANES), F32),
            pltpu.VMEM((tiles, 2 * EXPO_ROWS, LANES), F32),
            pltpu.VMEM((tiles, EXPO_ROWS, LANES), F32),
            pltpu.VMEM((2 * loops, 8, FC), F32),
            pltpu.VMEM((2 * loops, 8, FC), F32),
            pltpu.VMEM((tiles * loops, 4, LANES), F32),
            pltpu.VMEM((tiles * loops, 4, LANES), F32),
            pltpu.SemaphoreType.DMA((8,)),
            pltpu.SemaphoreType.DMA((8,)),
        ],
        compiler_params=pltpu.CompilerParams(
            collective_id=0, has_side_effects=True, vmem_limit_bytes=32 * 1024 * 1024
        ),
    )(star_slot, star_block, exposure, superpixel, magnitude, weight)
    return star.reshape(-1), expo.reshape(-1), flat


def solution(mesh):
    in_specs = (
        P("tile", "loop", None),
        P("tile", "loop"),
        P("tile", "loop", None),
        P("tile", "loop", None),
        P("tile", "loop", None),
        P("tile", "loop", None),
    )
    out_specs = (P(("tile", "loop")), P("loop"), P("tile", None))
    return jax.shard_map(
        functools.partial(on_device, mesh.shape["tile"], mesh.shape["loop"]),
        mesh=mesh, in_specs=in_specs, out_specs=out_specs, check_vma=False,
    )
```

```python
import functools

import jax
import jax.numpy as jnp
from jax import lax
from jax.experimental import pallas as pl
from jax.experimental.pallas import tpu as pltpu
from jax.sharding import PartitionSpec as P

FC = 256
ROWS_DEV = 8
SBLK_DEV = 2
EXP_DEV = 512
STAR_BLK = 256

SMOOTH = 2.0
RIDGE = 0.5

LANES = 128
HALF = LANES // 2
HALVES = FC // LANES
STAR_ROWS = SBLK_DEV * STAR_BLK // LANES
EXPO_ROWS = EXP_DEV // LANES
FLAT_ROWS = HALVES * ROWS_DEV
MESH = pl.DeviceIdType.MESH
F32 = jnp.float32
BF16 = jnp.bfloat16


def pieces(values):
    high = values.astype(BF16).astype(F32)
    return high, values - high


def fold(items):
    total = items[0]
    for item in items[1:]:
        total = total + item
    return total


def lane_fold(row):
    row = jnp.sum(row, axis=0, keepdims=True)
    return fold([row[:, at : at + LANES] for at in range(0, row.shape[1], LANES)])


def line(rows):
    return jnp.concatenate([rows[b : b + 1, :] for b in range(rows.shape[0])], axis=1)


def beside_columns(flat):
    column = lax.broadcasted_iota(jnp.int32, flat.shape, 1)
    left = jnp.where(column == 0, 0.0, pltpu.roll(flat, 1, 1))
    right = jnp.where(column == FC - 1, 0.0, pltpu.roll(flat, FC - 1, 1))
    return left + right


def kernel(
    tiles, loops,
    slot_in, block_in, expo_in, pixel_in, mag_in, weight_in,
    star_out, expo_out, flat_out,
    slot_ref, block_ref, expo_ref, pixel_ref, mag_ref, weight_ref, load,
    hot, mask, edges0, edges1, ext,
    loop0, loop1, expo0, expo1, halo0, halo1, dots0, dots1,
    send, recv,
):
    tile = lax.axis_index("tile")
    loop = lax.axis_index("loop")
    everyone = tiles * loops
    rank = tile * loops + loop
    blocks = slot_ref.shape[1]
    per_shard = blocks // loops
    star_wide = loops * STAR_ROWS
    star_rows = 2 * star_wide
    expo_at = star_rows
    flat_at = star_rows + 2 * EXPO_ROWS
    rows = flat_at + FLAT_ROWS

    loads = [
        pltpu.make_async_copy(src, dst, load.at[k])
        for k, (src, dst) in enumerate((
            (slot_in, slot_ref), (block_in, block_ref), (expo_in, expo_ref),
            (pixel_in, pixel_ref), (weight_in, weight_ref), (mag_in, mag_ref),
        ))
    ]
    for copy in loads:
        copy.start()

    def turn(index, d, size):
        index = index + d
        return jnp.where(index >= size, index - size, index)

    def each_other(act):
        for k in range(loops):
            to = turn(loop, k, loops)

            def step(d, carry, to=to):
                act((turn(tile, d, tiles), to))
                return carry

            lax.fori_loop(0 if k else 1, tiles, step, 0)

    barrier = pltpu.get_barrier_semaphore()
    each_other(
        lambda device: pl.semaphore_signal(barrier, inc=1, device_id=device, device_id_type=MESH)
    )

    def push(src, dst, which, device):
        pltpu.make_async_remote_copy(
            src_ref=src, dst_ref=dst, send_sem=send.at[which], recv_sem=recv.at[which],
            device_id=device, device_id_type=MESH,
        ).start()

    def settle(buffer, count, sem):
        part = buffer.at[pl.ds(0, count)]
        pltpu.make_async_copy(part, part, sem).wait()

    def push_tiles(buffer, which):
        def step(d, carry):
            push(buffer.at[tile], buffer.at[tile], which, (turn(tile, d, tiles), loop))
            return carry

        lax.fori_loop(1, tiles, step, 0)

    def push_loops(buffer, which):
        for d in range(1, loops):
            push(buffer.at[loop], buffer.at[loop], which, (tile, turn(loop, d, loops)))

    def push_edges(edges, buffer, which):
        above = turn(tile, tiles - 1, tiles)
        below = turn(tile, 1, tiles)
        for d in range(loops):
            to = turn(loop, d, loops)
            push(edges, buffer.at[loops + loop], which, (above, to))
            push(edges, buffer.at[loop], which, (below, to))

    def push_dots(buffer, which):
        each_other(lambda device: push(buffer.at[rank], buffer.at[rank], which, device))

    half_ids = lax.broadcasted_iota(jnp.int32, (HALF, LANES), 0)
    lane_ids = lax.broadcasted_iota(jnp.int32, (LANES, LANES), 0)
    star_ids = lax.broadcasted_iota(jnp.int32, (star_rows, LANES), 0)
    expo_ids = lax.broadcasted_iota(jnp.int32, (2 * EXPO_ROWS, LANES), 0)
    flat_ids = lax.broadcasted_iota(jnp.int32, (FLAT_ROWS, LANES), 0)
    for copy in loads:
        copy.wait()
    for b in range(blocks):
        at = slice(b * LANES, (b + 1) * LANES)
        star = block_ref[0, b] * STAR_BLK + slot_ref[0, b : b + 1, :]
        expo = expo_ref[0, b : b + 1, :]
        pixel = pixel_ref[0, b : b + 1, :]
        hot[0:HALF, at] = jnp.where(half_ids == (star & (HALF - 1)), 1.0, 0.0).astype(BF16)
        hot[HALF:LANES, at] = jnp.where(half_ids == (expo & (HALF - 1)), 1.0, 0.0).astype(BF16)
        hot[LANES : 2 * LANES, at] = jnp.where(lane_ids == (pixel & (LANES - 1)), 1.0, 0.0).astype(BF16)
        star_high = (
            (b // per_shard) * (2 * STAR_ROWS) + ((star // HALF) & 1) * STAR_ROWS + star // LANES
        )
        expo_high = ((expo // HALF) & 1) * EXPO_ROWS + expo // LANES
        pixel_high = (pixel // LANES) % HALVES * ROWS_DEV + pixel // FC
        mask[0:star_rows, at] = jnp.where(star_ids == star_high, 1.0, 0.0)
        mask[expo_at:flat_at, at] = jnp.where(expo_ids == expo_high, 1.0, 0.0)
        mask[flat_at:rows, at] = jnp.where(flat_ids == pixel_high, 1.0, 0.0)

    weights = line(weight_ref[0])
    weighted = weights * line(mag_ref[0])

    def lower(count):
        return lax.broadcasted_iota(jnp.int32, (count, LANES), 1) < HALF

    def swap(part):
        return pltpu.roll(part, HALF, 1)

    def scatter(*values):
        parts = jnp.concatenate(
            [mask[...] * piece for value in values for piece in pieces(value)], axis=0
        )
        sums = lax.dot_general(
            parts.astype(BF16), hot[...], (((1,), (1,)), ((), ())), preferred_element_type=F32
        )
        out = []
        for k in range(len(values)):
            both = sums[2 * k * rows : (2 * k + 1) * rows] + sums[(2 * k + 1) * rows : (2 * k + 2) * rows]
            left, flat = both[:, 0:LANES], both[flat_at:rows, LANES:]
            star = []
            for at in range(0, star_rows, 2 * STAR_ROWS):
                low = left[at : at + STAR_ROWS]
                high = left[at + STAR_ROWS : at + 2 * STAR_ROWS]
                star.append(jnp.where(lower(STAR_ROWS), low, swap(high)))
            low, high = left[expo_at : expo_at + EXPO_ROWS], left[expo_at + EXPO_ROWS : flat_at]
            out.append((
                jnp.concatenate(star, axis=0),
                jnp.where(lower(EXPO_ROWS), swap(low), high),
                jnp.concatenate(
                    [flat[h * ROWS_DEV : (h + 1) * ROWS_DEV] for h in range(HALVES)], axis=1
                ),
            ))
        return out

    def gather(star, expo, flat):
        parts = []
        for at in range(0, star_wide, STAR_ROWS):
            part = star[at : at + STAR_ROWS]
            parts += [part, swap(part)]
        star = jnp.where(lower(star_rows), jnp.concatenate(parts, axis=0), 0.0)
        expo = jnp.where(lower(2 * EXPO_ROWS), 0.0, jnp.concatenate([swap(expo), expo], axis=0))
        left = jnp.concatenate([star, expo, jnp.zeros((FLAT_ROWS, LANES), F32)], axis=0)
        right = jnp.concatenate(
            [jnp.zeros((flat_at, LANES), F32)]
            + [flat[:, h * LANES : (h + 1) * LANES] for h in range(HALVES)],
            axis=0,
        )
        values = jnp.concatenate([left, right], axis=1)
        found = jnp.dot(
            jnp.concatenate(pieces(values), axis=0).astype(BF16), hot[...],
            preferred_element_type=F32,
        )
        return jnp.sum((found[0:rows] + found[rows:]) * mask[...], axis=0, keepdims=True)

    (rhs, count) = scatter(weighted, weights)
    expo0[tile] = jnp.concatenate([rhs[1], count[1]], axis=0)
    loop0[loop] = jnp.concatenate(
        [rhs[0], count[0]]
        + [part[2][:, h * LANES : (h + 1) * LANES] for part in (rhs, count) for h in range(HALVES)],
        axis=0,
    )
    edges0[0:2] = rhs[2][0:2]
    edges0[2:4] = count[2][0:2]
    edges0[4:6] = rhs[2][ROWS_DEV - 2 :]
    edges0[6:8] = count[2][ROWS_DEV - 2 :]
    pl.semaphore_wait(barrier, everyone - 1)
    push_tiles(expo0, 0)
    push_edges(edges0, halo0, 2)
    push_loops(loop0, 1)

    settle(loop0, loops - 1, recv.at[1])
    joint = fold([loop0[l] for l in range(loops)])
    rhs_star = joint[0:star_wide]
    diag_star = joint[star_wide : 2 * star_wide] + RIDGE
    joint = joint[2 * star_wide :]
    rhs_mine, count_mine = [
        jnp.concatenate(
            [joint[(k * HALVES + h) * ROWS_DEV : (k * HALVES + h + 1) * ROWS_DEV] for h in range(HALVES)],
            axis=1,
        )
        for k in range(2)
    ]
    settle(halo0, 2 * loops, recv.at[2])
    over = fold([halo0[l] for l in range(loops)])
    under = fold([halo0[loops + l] for l in range(loops)])
    over = jnp.where(tile > 0, over, 0.0)
    under = jnp.where(tile < tiles - 1, under, 0.0)
    inner = slice(2, 2 + ROWS_DEV)
    wide = slice(1, 3 + ROWS_DEV)
    whole = slice(0, 4 + ROWS_DEV)
    ext[0, inner] = rhs_mine
    ext[0, 0:2] = over[4:6]
    ext[0, 2 + ROWS_DEV : 4 + ROWS_DEV] = under[0:2]
    ext[1, inner] = count_mine
    ext[1, 0:2] = over[6:8]
    ext[1, 2 + ROWS_DEV : 4 + ROWS_DEV] = under[2:4]
    ext[2, whole] = ext[0, whole] / (ext[1, whole] + (4.0 * SMOOTH + RIDGE))
    g_star = rhs_star / diag_star
    g_flat = ext[2, inner]
    settle(expo0, tiles - 1, recv.at[0])
    joint = fold([expo0[t] for t in range(tiles)])
    rhs_expo = joint[0:EXPO_ROWS]
    diag_expo = joint[EXPO_ROWS:] + RIDGE
    g_expo = rhs_expo / diag_expo

    shard_row = lax.broadcasted_iota(jnp.int32, (star_wide, LANES), 0) // STAR_ROWS
    own_star = jnp.where(shard_row == loop, 1.0, 0.0)
    own_expo = jnp.where(tile == 0, 1.0, 0.0)
    own_flat = jnp.where(loop == 0, 1.0, 0.0)

    def inner_rows(star, expo, flat):
        return (
            lane_fold(own_star * star) + own_expo * lane_fold(expo) + own_flat * lane_fold(flat)
        )

    fitted = gather(g_star, g_expo, g_flat)
    pulled = weights * fitted
    ((sum_star, sum_expo, sum_flat),) = scatter(pulled)
    expo1[tile, 0:EXPO_ROWS] = sum_expo
    loop1[loop] = jnp.concatenate(
        [sum_star] + [sum_flat[:, h * LANES : (h + 1) * LANES] for h in range(HALVES)], axis=0
    )
    edges1[0:1] = sum_flat[0:1]
    edges1[1:2] = sum_flat[ROWS_DEV - 1 :]
    push_tiles(expo1, 3)
    push_edges(edges1, halo1, 5)
    push_loops(loop1, 4)
    v = ext[2, wide]
    smooth = SMOOTH * (4.0 * v - ext[2, 0 : 2 + ROWS_DEV] - ext[2, 2 : 4 + ROWS_DEV] - beside_columns(v)) + RIDGE * v
    ext[3, wide] = smooth
    smooth_mine = ext[3, inner]
    dots0[rank, 0:1] = inner_rows(rhs_star * g_star, rhs_expo * g_expo, rhs_mine * g_flat)
    dots0[rank, 1:2] = lane_fold(pulled * fitted) + inner_rows(
        RIDGE * g_star * g_star, RIDGE * g_expo * g_expo, smooth_mine * g_flat
    )
    push_dots(dots0, 6)

    settle(loop1, loops - 1, recv.at[4])
    joint = fold([loop1[l] for l in range(loops)])
    image_star = joint[0:star_wide] + RIDGE * g_star
    sum_mine = jnp.concatenate(
        [joint[star_wide + h * ROWS_DEV : star_wide + (h + 1) * ROWS_DEV] for h in range(HALVES)], axis=1
    )
    settle(halo1, 2 * loops, recv.at[5])
    over = fold([halo1[l] for l in range(loops)])
    under = fold([halo1[loops + l] for l in range(loops)])
    ext[4, inner] = sum_mine
    ext[4, 1:2] = over[1:2]
    ext[4, 2 + ROWS_DEV : 3 + ROWS_DEV] = under[0:1]
    row = lax.broadcasted_iota(jnp.int32, (2 + ROWS_DEV, FC), 0)
    inside = ((row > 0) | (tile > 0)) & ((row < 1 + ROWS_DEV) | (tile < tiles - 1))
    image_wide = jnp.where(inside, ext[4, wide] + smooth, 0.0)
    settle(expo1, tiles - 1, recv.at[3])
    joint = fold([expo1[t, 0:EXPO_ROWS] for t in range(tiles)])
    image_expo = joint + RIDGE * g_expo

    def total(buffer, which, count):
        settle(buffer, everyone - 1, recv.at[which])
        joint = fold([buffer[r] for r in range(everyone)])
        return [jnp.sum(joint[k : k + 1], axis=1, keepdims=True) for k in range(count)]

    ext[7, wide] = image_wide
    fitted_image = gather(
        image_star / diag_star,
        image_expo / diag_expo,
        ext[7, inner] / (count_mine + (4.0 * SMOOTH + RIDGE)),
    )
    norm, curve = total(dots0, 6, 2)
    alpha = norm / curve

    res_star = rhs_star - alpha * image_star
    res_expo = rhs_expo - alpha * image_expo
    res_wide = ext[0, wide] - alpha * image_wide
    h_star = res_star / diag_star
    h_expo = res_expo / diag_expo
    ext[5, wide] = res_wide / (ext[1, wide] + (4.0 * SMOOTH + RIDGE))
    ext[6, wide] = res_wide
    h_flat = ext[5, inner]
    fitted = fitted - alpha * fitted_image
    beside = ext[5, 1 : 1 + ROWS_DEV] + ext[5, 3 : 3 + ROWS_DEV] + beside_columns(h_flat)
    dots1[rank, 0:1] = inner_rows(res_star * h_star, res_expo * h_expo, ext[6, inner] * h_flat)
    dots1[rank, 1:2] = inner_rows(image_star * h_star, image_expo * h_expo, ext[7, inner] * h_flat)
    dots1[rank, 2:3] = lane_fold(weights * fitted * fitted) + inner_rows(
        RIDGE * h_star * h_star,
        RIDGE * h_expo * h_expo,
        (SMOOTH * (4.0 * h_flat - beside) + RIDGE * h_flat) * h_flat,
    )
    push_dots(dots1, 7)
    norm_next, cross, curve_next = total(dots1, 7, 3)
    ratio = norm_next / norm
    step = norm_next / (curve_next + ratio * (2.0 * cross + ratio * curve))

    def solve(first, second):
        return alpha * first + step * (second + ratio * first)

    star = solve(g_star, h_star)
    star_out[...] = fold([
        jnp.where(loop == l, star[l * STAR_ROWS : (l + 1) * STAR_ROWS], 0.0) for l in range(loops)
    ])
    expo_out[...] = solve(g_expo, h_expo)
    flat_out[...] = solve(g_flat, h_flat)

    for which, (buffer, count) in enumerate((
        (expo0, tiles - 1), (loop0, loops - 1), (halo0, 2 * loops),
        (expo1, tiles - 1), (loop1, loops - 1), (halo1, 2 * loops),
        (dots0, everyone - 1), (dots1, everyone - 1),
    )):
        settle(buffer, count, send.at[which])


def write_kernel(star, expo, flat, star_out, expo_out, flat_out, sems):
    copies = [
        pltpu.make_async_copy(src, dst, sems.at[k])
        for k, (src, dst) in enumerate(((star, star_out), (expo, expo_out), (flat, flat_out)))
    ]
    for copy in copies:
        copy.start()
    for copy in copies:
        copy.wait()


def on_device(tiles, loops, star_slot, star_block, exposure, superpixel, magnitude, weight):
    blocks = star_slot.shape[1]
    seen = blocks * LANES
    star_wide = loops * STAR_ROWS
    rows = 2 * star_wide + 2 * EXPO_ROWS + FLAT_ROWS
    vmem = pl.BlockSpec(memory_space=pltpu.VMEM)
    hbm = pl.BlockSpec(memory_space=pltpu.HBM)
    out_shape = (
        jax.ShapeDtypeStruct((STAR_ROWS, LANES), F32),
        jax.ShapeDtypeStruct((EXPO_ROWS, LANES), F32),
        jax.ShapeDtypeStruct((ROWS_DEV, FC), F32),
    )
    parts = pl.pallas_call(
        functools.partial(kernel, tiles, loops),
        out_shape=out_shape,
        in_specs=[hbm] * 6,
        out_specs=(vmem, vmem, vmem),
        scratch_shapes=[
            pltpu.VMEM(star_slot.shape, jnp.int32),
            pltpu.SMEM(star_block.shape, jnp.int32),
            pltpu.VMEM(exposure.shape, jnp.int32),
            pltpu.VMEM(superpixel.shape, jnp.int32),
            pltpu.VMEM(magnitude.shape, F32),
            pltpu.VMEM(weight.shape, F32),
            pltpu.SemaphoreType.DMA((6,)),
            pltpu.VMEM((2 * LANES, seen), BF16),
            pltpu.VMEM((rows, seen), F32),
            pltpu.VMEM((8, FC), F32),
            pltpu.VMEM((8, FC), F32),
            pltpu.VMEM((8, ROWS_DEV + 8, FC), F32),
            pltpu.VMEM((loops, 2 * (star_wide + FLAT_ROWS), LANES), F32),
            pltpu.VMEM((loops, star_wide + FLAT_ROWS, LANES), F32),
            pltpu.VMEM((tiles, 2 * EXPO_ROWS, LANES), F32),
            pltpu.VMEM((tiles, EXPO_ROWS, LANES), F32),
            pltpu.VMEM((2 * loops, 8, FC), F32),
            pltpu.VMEM((2 * loops, 8, FC), F32),
            pltpu.VMEM((tiles * loops, 4, LANES), F32),
            pltpu.VMEM((tiles * loops, 4, LANES), F32),
            pltpu.SemaphoreType.DMA((8,)),
            pltpu.SemaphoreType.DMA((8,)),
        ],
        compiler_params=pltpu.CompilerParams(
            collective_id=0, has_side_effects=True, vmem_limit_bytes=32 * 1024 * 1024
        ),
    )(*[
        pltpu.with_memory_space_constraint(x, pltpu.HBM)
        for x in (star_slot, star_block, exposure, superpixel, magnitude, weight)
    ])
    star, expo, flat = pl.pallas_call(
        write_kernel,
        out_shape=out_shape,
        in_specs=[vmem] * 3,
        out_specs=(hbm,) * 3,
        scratch_shapes=[pltpu.SemaphoreType.DMA((3,))],
    )(*parts)
    return star.reshape(-1), expo.reshape(-1), flat


def solution(mesh):
    in_specs = (
        P("tile", "loop", None),
        P("tile", "loop"),
        P("tile", "loop", None),
        P("tile", "loop", None),
        P("tile", "loop", None),
        P("tile", "loop", None),
    )
    out_specs = (P(("tile", "loop")), P("loop"), P("tile", None))
    return jax.shard_map(
        functools.partial(on_device, mesh.shape["tile"], mesh.shape["loop"]),
        mesh=mesh, in_specs=in_specs, out_specs=out_specs, check_vma=False,
    )
```

```python
import functools

import jax
import jax.numpy as jnp
from jax import lax
from jax.experimental import pallas as pl
from jax.experimental.pallas import tpu as pltpu
from jax.sharding import PartitionSpec as P

FC = 256
ROWS_DEV = 8
SBLK_DEV = 2
EXP_DEV = 512
STAR_BLK = 256

SMOOTH = 2.0
RIDGE = 0.5

LANES = 128
HALF = LANES // 2
HALVES = FC // LANES
STAR_ROWS = SBLK_DEV * STAR_BLK // LANES
EXPO_ROWS = EXP_DEV // LANES
FLAT_ROWS = HALVES * ROWS_DEV
MESH = pl.DeviceIdType.MESH
F32 = jnp.float32
BF16 = jnp.bfloat16


def pieces(values):
    high = values.astype(BF16).astype(F32)
    return high, values - high


def fold(items):
    total = items[0]
    for item in items[1:]:
        total = total + item
    return total


def lane_fold(row):
    row = jnp.sum(row, axis=0, keepdims=True)
    return fold([row[:, at : at + LANES] for at in range(0, row.shape[1], LANES)])


def line(rows):
    return jnp.concatenate([rows[b : b + 1, :] for b in range(rows.shape[0])], axis=1)


def beside_columns(flat):
    column = lax.broadcasted_iota(jnp.int32, flat.shape, 1)
    left = jnp.where(column == 0, 0.0, pltpu.roll(flat, 1, 1))
    right = jnp.where(column == FC - 1, 0.0, pltpu.roll(flat, FC - 1, 1))
    return left + right


def kernel(
    tiles, loops,
    slot_in, block_in, expo_in, pixel_in, mag_in, weight_in,
    star_out, expo_out, flat_out,
    slot_ref, block_ref, expo_ref, pixel_ref, mag_ref, weight_ref, load,
    hot, mask, edges0, edges1, ext,
    loop0, loop1, wide0, wide1, expo0, expo1, halo0, halo1, dots0, dots1,
    send, recv,
):
    tile = lax.axis_index("tile")
    loop = lax.axis_index("loop")
    everyone = tiles * loops
    rank = tile * loops + loop
    blocks = slot_ref.shape[1]
    per_shard = blocks // loops
    star_wide = loops * STAR_ROWS
    star_rows = 2 * star_wide
    expo_at = star_rows
    flat_at = star_rows + 2 * EXPO_ROWS
    rows = flat_at + FLAT_ROWS

    loads = [
        pltpu.make_async_copy(src, dst, load.at[k])
        for k, (src, dst) in enumerate((
            (slot_in, slot_ref), (block_in, block_ref), (expo_in, expo_ref),
            (pixel_in, pixel_ref), (weight_in, weight_ref), (mag_in, mag_ref),
        ))
    ]
    for copy in loads:
        copy.start()

    def turn(index, d, size):
        index = index + d
        return jnp.where(index >= size, index - size, index)

    def span(first, last, act):
        if last <= 16:
            for d in range(first, last):
                act(d)
            return

        def step(d, carry):
            act(d)
            return carry

        lax.fori_loop(first, last, step, 0)

    def each_other(act):
        for k in range(loops):
            to = turn(loop, k, loops)

            span(0 if k else 1, tiles, lambda d, to=to: act((turn(tile, d, tiles), to)))

    barrier = pltpu.get_barrier_semaphore()
    each_other(
        lambda device: pl.semaphore_signal(barrier, inc=1, device_id=device, device_id_type=MESH)
    )

    def push(src, dst, which, device):
        pltpu.make_async_remote_copy(
            src_ref=src, dst_ref=dst, send_sem=send.at[which], recv_sem=recv.at[which],
            device_id=device, device_id_type=MESH,
        ).start()

    def settle(buffer, count, sem):
        part = buffer.at[pl.ds(0, count)]
        pltpu.make_async_copy(part, part, sem).wait()

    def push_tiles(buffer, which):
        span(1, tiles, lambda d: push(
            buffer.at[tile], buffer.at[tile], which, (turn(tile, d, tiles), loop)
        ))

    def push_loops(buffer, which):
        for d in range(1, loops):
            push(buffer.at[loop], buffer.at[loop], which, (tile, turn(loop, d, loops)))

    def push_edges(edges, buffer, which):
        above = turn(tile, tiles - 1, tiles)
        below = turn(tile, 1, tiles)
        for d in range(loops):
            to = turn(loop, d, loops)
            push(edges, buffer.at[loops + loop], which, (above, to))
            push(edges, buffer.at[loop], which, (below, to))

    def push_dots(buffer, which):
        each_other(lambda device: push(buffer.at[rank], buffer.at[rank], which, device))

    half_ids = lax.broadcasted_iota(jnp.int32, (HALF, LANES), 0)
    lane_ids = lax.broadcasted_iota(jnp.int32, (LANES, LANES), 0)
    star_ids = lax.broadcasted_iota(jnp.int32, (star_rows, LANES), 0)
    expo_ids = lax.broadcasted_iota(jnp.int32, (2 * EXPO_ROWS, LANES), 0)
    flat_ids = lax.broadcasted_iota(jnp.int32, (FLAT_ROWS, LANES), 0)
    for copy in loads:
        copy.wait()
    for b in range(blocks):
        at = slice(b * LANES, (b + 1) * LANES)
        star = block_ref[0, b] * STAR_BLK + slot_ref[0, b : b + 1, :]
        expo = expo_ref[0, b : b + 1, :]
        pixel = pixel_ref[0, b : b + 1, :]
        hot[0:HALF, at] = jnp.where(half_ids == (star & (HALF - 1)), 1.0, 0.0).astype(BF16)
        hot[HALF:LANES, at] = jnp.where(half_ids == (expo & (HALF - 1)), 1.0, 0.0).astype(BF16)
        hot[LANES : 2 * LANES, at] = jnp.where(lane_ids == (pixel & (LANES - 1)), 1.0, 0.0).astype(BF16)
        star_high = (
            (b // per_shard) * (2 * STAR_ROWS) + ((star // HALF) & 1) * STAR_ROWS + star // LANES
        )
        expo_high = ((expo // HALF) & 1) * EXPO_ROWS + expo // LANES
        pixel_high = (pixel // LANES) % HALVES * ROWS_DEV + pixel // FC
        mask[0:star_rows, at] = jnp.where(star_ids == star_high, 1.0, 0.0)
        mask[expo_at:flat_at, at] = jnp.where(expo_ids == expo_high, 1.0, 0.0)
        mask[flat_at:rows, at] = jnp.where(flat_ids == pixel_high, 1.0, 0.0)

    weights = line(weight_ref[0])
    weighted = weights * line(mag_ref[0])

    def lower(count):
        return lax.broadcasted_iota(jnp.int32, (count, LANES), 1) < HALF

    def swap(part):
        return pltpu.roll(part, HALF, 1)

    def spread(values, mine, columns):
        parts = jnp.concatenate(
            [mask[mine] * piece for value in values for piece in pieces(value)], axis=0
        )
        sums = lax.dot_general(
            parts.astype(BF16), hot[columns], (((1,), (1,)), ((), ())), preferred_element_type=F32
        )
        size = mine.stop - mine.start
        return [
            sums[2 * k * size : (2 * k + 1) * size] + sums[(2 * k + 1) * size : (2 * k + 2) * size]
            for k in range(len(values))
        ]

    near = slice(0, flat_at)
    far = slice(flat_at, rows)
    near_columns = slice(0, LANES)
    far_columns = slice(LANES, 2 * LANES)

    def scatter_near(*values):
        out = []
        for left in spread(values, near, near_columns):
            star = []
            for at in range(0, star_rows, 2 * STAR_ROWS):
                low = left[at : at + STAR_ROWS]
                high = left[at + STAR_ROWS : at + 2 * STAR_ROWS]
                star.append(jnp.where(lower(STAR_ROWS), low, swap(high)))
            low, high = left[expo_at : expo_at + EXPO_ROWS], left[expo_at + EXPO_ROWS : flat_at]
            out.append((
                jnp.concatenate(star, axis=0), jnp.where(lower(EXPO_ROWS), swap(low), high)
            ))
        return out

    def scatter_flat(*values):
        return spread(values, far, far_columns)

    def in_lines(flat):
        return jnp.concatenate(
            [flat[h * ROWS_DEV : (h + 1) * ROWS_DEV] for h in range(HALVES)], axis=1
        )

    def find(values, mine, columns):
        size = mine.stop - mine.start
        found = jnp.dot(
            jnp.concatenate(pieces(values), axis=0).astype(BF16), hot[columns],
            preferred_element_type=F32,
        )
        return jnp.sum((found[0:size] + found[size:]) * mask[mine], axis=0, keepdims=True)

    def gather_near(star, expo):
        parts = []
        for at in range(0, star_wide, STAR_ROWS):
            part = star[at : at + STAR_ROWS]
            parts += [part, swap(part)]
        star = jnp.where(lower(star_rows), jnp.concatenate(parts, axis=0), 0.0)
        expo = jnp.where(lower(2 * EXPO_ROWS), 0.0, jnp.concatenate([swap(expo), expo], axis=0))
        return find(jnp.concatenate([star, expo], axis=0), near, near_columns)

    def gather_flat(flat):
        halves = [flat[:, h * LANES : (h + 1) * LANES] for h in range(HALVES)]
        return find(jnp.concatenate(halves, axis=0), far, far_columns)

    quarter = lax.broadcasted_iota(jnp.int32, (1, LANES), 1) // (LANES // 4)

    def pack(*parts):
        both = jnp.concatenate(parts, axis=0)
        both = both + pltpu.roll(both, HALF, 1)
        both = both + pltpu.roll(both, HALF // 2, 1)
        row = both[0:1]
        for k in range(1, len(parts)):
            row = jnp.where(quarter == k, both[k : k + 1], row)
        return row

    (rhs, count) = scatter_near(weighted, weights)
    expo0[tile] = jnp.concatenate([rhs[1], count[1]], axis=0)
    loop0[loop] = jnp.concatenate([rhs[0], count[0]], axis=0)
    pl.semaphore_wait(barrier, everyone - 1)
    push_tiles(expo0, 0)
    push_loops(loop0, 1)
    (rhs, count) = scatter_flat(weighted, weights)
    wide0[loop] = jnp.concatenate([rhs, count], axis=0)
    rhs, count = in_lines(rhs), in_lines(count)
    edges0[0:2] = rhs[0:2]
    edges0[2:4] = count[0:2]
    edges0[4:6] = rhs[ROWS_DEV - 2 :]
    edges0[6:8] = count[ROWS_DEV - 2 :]
    push_edges(edges0, halo0, 2)
    push_loops(wide0, 8)

    settle(loop0, loops - 1, recv.at[1])
    joint = fold([loop0[l] for l in range(loops)])
    rhs_star = joint[0:star_wide]
    diag_star = joint[star_wide : 2 * star_wide] + RIDGE
    settle(wide0, loops - 1, recv.at[8])
    joint = fold([wide0[l] for l in range(loops)])
    rhs_mine = in_lines(joint[0:FLAT_ROWS])
    count_mine = in_lines(joint[FLAT_ROWS:])
    settle(halo0, 2 * loops, recv.at[2])
    over = fold([halo0[l] for l in range(loops)])
    under = fold([halo0[loops + l] for l in range(loops)])
    over = jnp.where(tile > 0, over, 0.0)
    under = jnp.where(tile < tiles - 1, under, 0.0)
    inner = slice(2, 2 + ROWS_DEV)
    wide = slice(1, 3 + ROWS_DEV)
    whole = slice(0, 4 + ROWS_DEV)
    ext[0, inner] = rhs_mine
    ext[0, 0:2] = over[4:6]
    ext[0, 2 + ROWS_DEV : 4 + ROWS_DEV] = under[0:2]
    ext[1, inner] = count_mine
    ext[1, 0:2] = over[6:8]
    ext[1, 2 + ROWS_DEV : 4 + ROWS_DEV] = under[2:4]
    ext[2, whole] = ext[0, whole] / (ext[1, whole] + (4.0 * SMOOTH + RIDGE))
    g_star = rhs_star / diag_star
    g_flat = ext[2, inner]
    fitted = gather_flat(g_flat)
    settle(expo0, tiles - 1, recv.at[0])
    joint = fold([expo0[t] for t in range(tiles)])
    rhs_expo = joint[0:EXPO_ROWS]
    diag_expo = joint[EXPO_ROWS:] + RIDGE
    g_expo = rhs_expo / diag_expo

    shard_row = lax.broadcasted_iota(jnp.int32, (star_wide, LANES), 0) // STAR_ROWS
    own_star = jnp.where(shard_row == loop, 1.0, 0.0)
    own_expo = jnp.where(tile == 0, 1.0, 0.0)
    own_flat = jnp.where(loop == 0, 1.0, 0.0)

    def inner_rows(star, expo, flat):
        return (
            lane_fold(own_star * star) + own_expo * lane_fold(expo) + own_flat * lane_fold(flat)
        )

    fitted = fitted + gather_near(g_star, g_expo)
    pulled = weights * fitted
    ((sum_star, sum_expo),) = scatter_near(pulled)
    expo1[tile] = sum_expo
    loop1[loop] = sum_star
    push_tiles(expo1, 3)
    push_loops(loop1, 4)
    (sum_flat,) = scatter_flat(pulled)
    wide1[loop] = sum_flat
    sum_flat = in_lines(sum_flat)
    edges1[0:1] = sum_flat[0:1]
    edges1[1:2] = sum_flat[ROWS_DEV - 1 :]
    push_edges(edges1, halo1, 5)
    push_loops(wide1, 9)
    v = ext[2, wide]
    smooth = SMOOTH * (4.0 * v - ext[2, 0 : 2 + ROWS_DEV] - ext[2, 2 : 4 + ROWS_DEV] - beside_columns(v)) + RIDGE * v
    ext[3, wide] = smooth
    smooth_mine = ext[3, inner]
    dots0[rank] = pack(
        inner_rows(rhs_star * g_star, rhs_expo * g_expo, rhs_mine * g_flat),
        lane_fold(pulled * fitted) + inner_rows(
            RIDGE * g_star * g_star, RIDGE * g_expo * g_expo, smooth_mine * g_flat
        ),
    )
    push_dots(dots0, 6)

    settle(loop1, loops - 1, recv.at[4])
    joint = fold([loop1[l] for l in range(loops)])
    image_star = joint + RIDGE * g_star
    settle(wide1, loops - 1, recv.at[9])
    sum_mine = in_lines(fold([wide1[l] for l in range(loops)]))
    settle(halo1, 2 * loops, recv.at[5])
    over = fold([halo1[l] for l in range(loops)])
    under = fold([halo1[loops + l] for l in range(loops)])
    ext[4, inner] = sum_mine
    ext[4, 1:2] = over[1:2]
    ext[4, 2 + ROWS_DEV : 3 + ROWS_DEV] = under[0:1]
    row = lax.broadcasted_iota(jnp.int32, (2 + ROWS_DEV, FC), 0)
    inside = ((row > 0) | (tile > 0)) & ((row < 1 + ROWS_DEV) | (tile < tiles - 1))
    image_wide = jnp.where(inside, ext[4, wide] + smooth, 0.0)
    ext[7, wide] = image_wide
    fitted_image = gather_flat(ext[7, inner] / (count_mine + (4.0 * SMOOTH + RIDGE)))
    settle(expo1, tiles - 1, recv.at[3])
    joint = fold([expo1[t] for t in range(tiles)])
    image_expo = joint + RIDGE * g_expo

    def total(buffer, which, count):
        settle(buffer, everyone - 1, recv.at[which])
        joint = fold([buffer[r] for r in range(everyone)])
        return [
            jnp.sum(jnp.where(quarter == k, joint, 0.0), axis=1, keepdims=True)
            for k in range(count)
        ]

    fitted_image = fitted_image + gather_near(image_star / diag_star, image_expo / diag_expo)
    norm, curve = total(dots0, 6, 2)
    alpha = norm / curve

    res_star = rhs_star - alpha * image_star
    res_expo = rhs_expo - alpha * image_expo
    res_wide = ext[0, wide] - alpha * image_wide
    h_star = res_star / diag_star
    h_expo = res_expo / diag_expo
    ext[5, wide] = res_wide / (ext[1, wide] + (4.0 * SMOOTH + RIDGE))
    ext[6, wide] = res_wide
    h_flat = ext[5, inner]
    fitted = fitted - alpha * fitted_image
    beside = ext[5, 1 : 1 + ROWS_DEV] + ext[5, 3 : 3 + ROWS_DEV] + beside_columns(h_flat)
    dots1[rank] = pack(
        inner_rows(res_star * h_star, res_expo * h_expo, ext[6, inner] * h_flat),
        inner_rows(image_star * h_star, image_expo * h_expo, ext[7, inner] * h_flat),
        lane_fold(weights * fitted * fitted) + inner_rows(
            RIDGE * h_star * h_star,
            RIDGE * h_expo * h_expo,
            (SMOOTH * (4.0 * h_flat - beside) + RIDGE * h_flat) * h_flat,
        ),
    )
    push_dots(dots1, 7)
    norm_next, cross, curve_next = total(dots1, 7, 3)
    ratio = norm_next / norm
    step = norm_next / (curve_next + ratio * (2.0 * cross + ratio * curve))

    def solve(first, second):
        return alpha * first + step * (second + ratio * first)

    star = solve(g_star, h_star)
    star_out[...] = fold([
        jnp.where(loop == l, star[l * STAR_ROWS : (l + 1) * STAR_ROWS], 0.0) for l in range(loops)
    ])
    expo_out[...] = solve(g_expo, h_expo)
    flat_out[...] = solve(g_flat, h_flat)

    for which, (buffer, count) in enumerate((
        (expo0, tiles - 1), (loop0, loops - 1), (halo0, 2 * loops),
        (expo1, tiles - 1), (loop1, loops - 1), (halo1, 2 * loops),
        (dots0, everyone - 1), (dots1, everyone - 1), (wide0, loops - 1), (wide1, loops - 1),
    )):
        settle(buffer, count, send.at[which])


def write_kernel(star, expo, flat, star_out, expo_out, flat_out, sems):
    copies = [
        pltpu.make_async_copy(src, dst, sems.at[k])
        for k, (src, dst) in enumerate(((star, star_out), (expo, expo_out), (flat, flat_out)))
    ]
    for copy in copies:
        copy.start()
    for copy in copies:
        copy.wait()


def on_device(tiles, loops, star_slot, star_block, exposure, superpixel, magnitude, weight):
    blocks = star_slot.shape[1]
    seen = blocks * LANES
    star_wide = loops * STAR_ROWS
    rows = 2 * star_wide + 2 * EXPO_ROWS + FLAT_ROWS
    vmem = pl.BlockSpec(memory_space=pltpu.VMEM)
    hbm = pl.BlockSpec(memory_space=pltpu.HBM)
    out_shape = (
        jax.ShapeDtypeStruct((STAR_ROWS, LANES), F32),
        jax.ShapeDtypeStruct((EXPO_ROWS, LANES), F32),
        jax.ShapeDtypeStruct((ROWS_DEV, FC), F32),
    )
    parts = pl.pallas_call(
        functools.partial(kernel, tiles, loops),
        out_shape=tuple(pltpu.VMEM(x.shape, x.dtype) for x in out_shape),
        in_specs=[hbm] * 6,
        out_specs=(vmem, vmem, vmem),
        scratch_shapes=[
            pltpu.VMEM(star_slot.shape, jnp.int32),
            pltpu.SMEM(star_block.shape, jnp.int32),
            pltpu.VMEM(exposure.shape, jnp.int32),
            pltpu.VMEM(superpixel.shape, jnp.int32),
            pltpu.VMEM(magnitude.shape, F32),
            pltpu.VMEM(weight.shape, F32),
            pltpu.SemaphoreType.DMA((6,)),
            pltpu.VMEM((2 * LANES, seen), BF16),
            pltpu.VMEM((rows, seen), F32),
            pltpu.VMEM((8, FC), F32),
            pltpu.VMEM((2, FC), F32),
            pltpu.VMEM((8, ROWS_DEV + 8, FC), F32),
            pltpu.VMEM((loops, 2 * star_wide, LANES), F32),
            pltpu.VMEM((loops, star_wide, LANES), F32),
            pltpu.VMEM((loops, 2 * FLAT_ROWS, LANES), F32),
            pltpu.VMEM((loops, FLAT_ROWS, LANES), F32),
            pltpu.VMEM((tiles, 2 * EXPO_ROWS, LANES), F32),
            pltpu.VMEM((tiles, EXPO_ROWS, LANES), F32),
            pltpu.VMEM((2 * loops, 8, FC), F32),
            pltpu.VMEM((2 * loops, 2, FC), F32),
            pltpu.VMEM((tiles * loops, 1, LANES), F32),
            pltpu.VMEM((tiles * loops, 1, LANES), F32),
            pltpu.SemaphoreType.DMA((10,)),
            pltpu.SemaphoreType.DMA((10,)),
        ],
        compiler_params=pltpu.CompilerParams(
            collective_id=0, has_side_effects=True, vmem_limit_bytes=32 * 1024 * 1024
        ),
    )(*[
        pltpu.with_memory_space_constraint(x, pltpu.HBM)
        for x in (star_slot, star_block, exposure, superpixel, magnitude, weight)
    ])
    star, expo, flat = pl.pallas_call(
        write_kernel,
        out_shape=out_shape,
        in_specs=[vmem] * 3,
        out_specs=(hbm,) * 3,
        scratch_shapes=[pltpu.SemaphoreType.DMA((3,))],
    )(*parts)
    return star.reshape(-1), expo.reshape(-1), flat


def solution(mesh):
    in_specs = (
        P("tile", "loop", None),
        P("tile", "loop"),
        P("tile", "loop", None),
        P("tile", "loop", None),
        P("tile", "loop", None),
        P("tile", "loop", None),
    )
    out_specs = (P(("tile", "loop")), P("loop"), P("tile", None))
    return jax.shard_map(
        functools.partial(on_device, mesh.shape["tile"], mesh.shape["loop"]),
        mesh=mesh, in_specs=in_specs, out_specs=out_specs, check_vma=False,
    )
```

```python
import functools

import jax
import jax.numpy as jnp
from jax import lax
from jax.experimental import pallas as pl
from jax.experimental.pallas import tpu as pltpu
from jax.sharding import PartitionSpec as P

FC = 256
ROWS_DEV = 8
SBLK_DEV = 2
EXP_DEV = 512
STAR_BLK = 256

SMOOTH = 2.0
RIDGE = 0.5

LANES = 128
HALF = LANES // 2
HALVES = FC // LANES
STAR_ROWS = SBLK_DEV * STAR_BLK // LANES
EXPO_ROWS = EXP_DEV // LANES
FLAT_ROWS = HALVES * ROWS_DEV
MESH = pl.DeviceIdType.MESH
F32 = jnp.float32
BF16 = jnp.bfloat16


def pieces(values):
    high = values.astype(BF16).astype(F32)
    return high, values - high


def fold(items):
    total = items[0]
    for item in items[1:]:
        total = total + item
    return total


def lane_fold(row):
    row = jnp.sum(row, axis=0, keepdims=True)
    return fold([row[:, at : at + LANES] for at in range(0, row.shape[1], LANES)])


def line(rows):
    return jnp.concatenate([rows[b : b + 1, :] for b in range(rows.shape[0])], axis=1)


def beside_columns(flat):
    column = lax.broadcasted_iota(jnp.int32, flat.shape, 1)
    left = jnp.where(column == 0, 0.0, pltpu.roll(flat, 1, 1))
    right = jnp.where(column == FC - 1, 0.0, pltpu.roll(flat, FC - 1, 1))
    return left + right


def kernel(
    tiles, loops,
    slot_in, block_in, expo_in, pixel_in, mag_in, weight_in,
    star_out, expo_out, flat_out,
    slot_ref, block_ref, expo_ref, pixel_ref, mag_ref, weight_ref, load,
    hot, mask, edges0, edges1, ext,
    loop0, loop1, wide0, wide1, expo0, expo1, halo0, halo1, dots0, dots1,
    send, recv,
):
    tile = lax.axis_index("tile")
    loop = lax.axis_index("loop")
    everyone = tiles * loops
    rank = tile * loops + loop
    blocks = slot_ref.shape[1]
    per_shard = blocks // loops
    star_wide = loops * STAR_ROWS
    star_rows = 2 * star_wide
    expo_at = star_rows
    flat_at = star_rows + 2 * EXPO_ROWS
    rows = flat_at + FLAT_ROWS

    loads = [
        pltpu.make_async_copy(src, dst, load.at[k])
        for k, (src, dst) in enumerate((
            (slot_in, slot_ref), (block_in, block_ref), (expo_in, expo_ref),
            (pixel_in, pixel_ref), (weight_in, weight_ref), (mag_in, mag_ref),
        ))
    ]
    for copy in loads:
        copy.start()

    def turn(index, d, size):
        index = index + d
        return jnp.where(index >= size, index - size, index)

    def span(first, last, act):
        if last <= 16:
            for d in range(first, last):
                act(d)
            return

        def step(d, carry):
            act(d)
            return carry

        lax.fori_loop(first, last, step, 0)

    def each_other(act):
        for k in range(loops):
            to = turn(loop, k, loops)

            span(0 if k else 1, tiles, lambda d, to=to: act((turn(tile, d, tiles), to)))

    barrier = pltpu.get_barrier_semaphore()
    each_other(
        lambda device: pl.semaphore_signal(barrier, inc=1, device_id=device, device_id_type=MESH)
    )

    def push(src, dst, which, device):
        pltpu.make_async_remote_copy(
            src_ref=src, dst_ref=dst, send_sem=send.at[which], recv_sem=recv.at[which],
            device_id=device, device_id_type=MESH,
        ).start()

    def settle(buffer, count, sem):
        part = buffer.at[pl.ds(0, count)]
        pltpu.make_async_copy(part, part, sem).wait()

    def push_tiles(buffer, which):
        span(1, tiles, lambda d: push(
            buffer.at[tile], buffer.at[tile], which, (turn(tile, d, tiles), loop)
        ))

    def push_loops(buffer, which):
        for d in range(1, loops):
            push(buffer.at[loop], buffer.at[loop], which, (tile, turn(loop, d, loops)))

    def push_edges(edges, buffer, which):
        above = turn(tile, tiles - 1, tiles)
        below = turn(tile, 1, tiles)
        for d in range(loops):
            to = turn(loop, d, loops)
            push(edges, buffer.at[loops + loop], which, (above, to))
            push(edges, buffer.at[loop], which, (below, to))

    def push_dots(buffer, which):
        each_other(lambda device: push(buffer.at[rank], buffer.at[rank], which, device))

    half_ids = lax.broadcasted_iota(jnp.int32, (HALF, LANES), 0)
    lane_ids = lax.broadcasted_iota(jnp.int32, (LANES, LANES), 0)
    star_ids = lax.broadcasted_iota(jnp.int32, (star_rows, LANES), 0)
    expo_ids = lax.broadcasted_iota(jnp.int32, (2 * EXPO_ROWS, LANES), 0)
    flat_ids = lax.broadcasted_iota(jnp.int32, (FLAT_ROWS, LANES), 0)
    for copy in loads:
        copy.wait()
    for b in range(blocks):
        at = slice(b * LANES, (b + 1) * LANES)
        star = block_ref[0, b] * STAR_BLK + slot_ref[0, b : b + 1, :]
        expo = expo_ref[0, b : b + 1, :]
        hot[0:HALF, at] = jnp.where(half_ids == (star & (HALF - 1)), 1.0, 0.0).astype(BF16)
        hot[HALF:LANES, at] = jnp.where(half_ids == (expo & (HALF - 1)), 1.0, 0.0).astype(BF16)
        star_high = (
            (b // per_shard) * (2 * STAR_ROWS) + ((star // HALF) & 1) * STAR_ROWS + star // LANES
        )
        expo_high = ((expo // HALF) & 1) * EXPO_ROWS + expo // LANES
        mask[0:star_rows, at] = jnp.where(star_ids == star_high, 1.0, 0.0)
        mask[expo_at:flat_at, at] = jnp.where(expo_ids == expo_high, 1.0, 0.0)

    weights = line(weight_ref[0])
    weighted = weights * line(mag_ref[0])

    def lower(count):
        return lax.broadcasted_iota(jnp.int32, (count, LANES), 1) < HALF

    def swap(part):
        return pltpu.roll(part, HALF, 1)

    def spread(values, mine, columns):
        parts = jnp.concatenate(
            [mask[mine] * piece for value in values for piece in pieces(value)], axis=0
        )
        sums = lax.dot_general(
            parts.astype(BF16), hot[columns], (((1,), (1,)), ((), ())), preferred_element_type=F32
        )
        size = mine.stop - mine.start
        return [
            sums[2 * k * size : (2 * k + 1) * size] + sums[(2 * k + 1) * size : (2 * k + 2) * size]
            for k in range(len(values))
        ]

    near = slice(0, flat_at)
    far = slice(flat_at, rows)
    near_columns = slice(0, LANES)
    far_columns = slice(LANES, 2 * LANES)

    def scatter_near(*values):
        out = []
        for left in spread(values, near, near_columns):
            star = []
            for at in range(0, star_rows, 2 * STAR_ROWS):
                low = left[at : at + STAR_ROWS]
                high = left[at + STAR_ROWS : at + 2 * STAR_ROWS]
                star.append(jnp.where(lower(STAR_ROWS), low, swap(high)))
            low, high = left[expo_at : expo_at + EXPO_ROWS], left[expo_at + EXPO_ROWS : flat_at]
            out.append((
                jnp.concatenate(star, axis=0), jnp.where(lower(EXPO_ROWS), swap(low), high)
            ))
        return out

    def scatter_flat(*values):
        return spread(values, far, far_columns)

    def in_lines(flat):
        return jnp.concatenate(
            [flat[h * ROWS_DEV : (h + 1) * ROWS_DEV] for h in range(HALVES)], axis=1
        )

    def find(values, mine, columns):
        size = mine.stop - mine.start
        found = jnp.dot(
            jnp.concatenate(pieces(values), axis=0).astype(BF16), hot[columns],
            preferred_element_type=F32,
        )
        return jnp.sum((found[0:size] + found[size:]) * mask[mine], axis=0, keepdims=True)

    def gather_near(star, expo):
        parts = []
        for at in range(0, star_wide, STAR_ROWS):
            part = star[at : at + STAR_ROWS]
            parts += [part, swap(part)]
        star = jnp.where(lower(star_rows), jnp.concatenate(parts, axis=0), 0.0)
        expo = jnp.where(lower(2 * EXPO_ROWS), 0.0, jnp.concatenate([swap(expo), expo], axis=0))
        return find(jnp.concatenate([star, expo], axis=0), near, near_columns)

    def gather_flat(flat):
        halves = [flat[:, h * LANES : (h + 1) * LANES] for h in range(HALVES)]
        return find(jnp.concatenate(halves, axis=0), far, far_columns)

    quarter = lax.broadcasted_iota(jnp.int32, (1, LANES), 1) // (LANES // 4)

    def pack(*parts):
        both = jnp.concatenate(parts, axis=0)
        both = both + pltpu.roll(both, HALF, 1)
        both = both + pltpu.roll(both, HALF // 2, 1)
        row = both[0:1]
        for k in range(1, len(parts)):
            row = jnp.where(quarter == k, both[k : k + 1], row)
        return row

    (rhs, count) = scatter_near(weighted, weights)
    expo0[tile] = jnp.concatenate([rhs[1], count[1]], axis=0)
    loop0[loop] = jnp.concatenate([rhs[0], count[0]], axis=0)
    pl.semaphore_wait(barrier, everyone - 1)
    push_tiles(expo0, 0)
    push_loops(loop0, 1)
    for b in range(blocks):
        at = slice(b * LANES, (b + 1) * LANES)
        pixel = pixel_ref[0, b : b + 1, :]
        hot[LANES : 2 * LANES, at] = jnp.where(lane_ids == (pixel & (LANES - 1)), 1.0, 0.0).astype(BF16)
        pixel_high = (pixel // LANES) % HALVES * ROWS_DEV + pixel // FC
        mask[flat_at:rows, at] = jnp.where(flat_ids == pixel_high, 1.0, 0.0)
    (rhs, count) = scatter_flat(weighted, weights)
    wide0[loop] = jnp.concatenate([rhs, count], axis=0)
    rhs, count = in_lines(rhs), in_lines(count)
    edges0[0:2] = rhs[0:2]
    edges0[2:4] = count[0:2]
    edges0[4:6] = rhs[ROWS_DEV - 2 :]
    edges0[6:8] = count[ROWS_DEV - 2 :]
    push_edges(edges0, halo0, 2)
    push_loops(wide0, 8)

    settle(loop0, loops - 1, recv.at[1])
    joint = fold([loop0[l] for l in range(loops)])
    rhs_star = joint[0:star_wide]
    diag_star = joint[star_wide : 2 * star_wide] + RIDGE
    settle(wide0, loops - 1, recv.at[8])
    joint = fold([wide0[l] for l in range(loops)])
    rhs_mine = in_lines(joint[0:FLAT_ROWS])
    count_mine = in_lines(joint[FLAT_ROWS:])
    settle(halo0, 2 * loops, recv.at[2])
    over = fold([halo0[l] for l in range(loops)])
    under = fold([halo0[loops + l] for l in range(loops)])
    over = jnp.where(tile > 0, over, 0.0)
    under = jnp.where(tile < tiles - 1, under, 0.0)
    inner = slice(2, 2 + ROWS_DEV)
    wide = slice(1, 3 + ROWS_DEV)
    whole = slice(0, 4 + ROWS_DEV)
    ext[0, inner] = rhs_mine
    ext[0, 0:2] = over[4:6]
    ext[0, 2 + ROWS_DEV : 4 + ROWS_DEV] = under[0:2]
    ext[1, inner] = count_mine
    ext[1, 0:2] = over[6:8]
    ext[1, 2 + ROWS_DEV : 4 + ROWS_DEV] = under[2:4]
    ext[2, whole] = ext[0, whole] / (ext[1, whole] + (4.0 * SMOOTH + RIDGE))
    g_star = rhs_star / diag_star
    g_flat = ext[2, inner]
    fitted = gather_flat(g_flat)
    shard_row = lax.broadcasted_iota(jnp.int32, (star_wide, LANES), 0) // STAR_ROWS
    own_star = jnp.where(shard_row == loop, 1.0, 0.0)
    own_expo = jnp.where(tile == 0, 1.0, 0.0)
    own_flat = jnp.where(loop == 0, 1.0, 0.0)

    def inner_rows(star, expo, flat):
        return (
            lane_fold(own_star * star) + own_expo * lane_fold(expo) + own_flat * lane_fold(flat)
        )

    v = ext[2, wide]
    smooth = SMOOTH * (4.0 * v - ext[2, 0 : 2 + ROWS_DEV] - ext[2, 2 : 4 + ROWS_DEV] - beside_columns(v)) + RIDGE * v
    ext[3, wide] = smooth
    smooth_mine = ext[3, inner]
    norm = lane_fold(own_star * rhs_star * g_star) + own_flat * lane_fold(rhs_mine * g_flat)
    curve = RIDGE * lane_fold(own_star * g_star * g_star) + own_flat * lane_fold(smooth_mine * g_flat)
    settle(expo0, tiles - 1, recv.at[0])
    joint = fold([expo0[t] for t in range(tiles)])
    rhs_expo = joint[0:EXPO_ROWS]
    diag_expo = joint[EXPO_ROWS:] + RIDGE
    g_expo = rhs_expo / diag_expo

    fitted = fitted + gather_near(g_star, g_expo)
    pulled = weights * fitted
    ((sum_star, sum_expo),) = scatter_near(pulled)
    expo1[tile, 0:EXPO_ROWS] = sum_expo
    expo1[tile, EXPO_ROWS : EXPO_ROWS + 1] = pack(
        norm + own_expo * lane_fold(rhs_expo * g_expo),
        curve + lane_fold(pulled * fitted) + (own_expo * RIDGE) * lane_fold(g_expo * g_expo),
    )
    loop1[loop] = sum_star
    push_tiles(expo1, 3)
    push_loops(loop1, 4)
    (sum_flat,) = scatter_flat(pulled)
    wide1[loop] = sum_flat
    sum_flat = in_lines(sum_flat)
    edges1[0:1] = sum_flat[0:1]
    edges1[1:2] = sum_flat[ROWS_DEV - 1 :]
    push_edges(edges1, halo1, 5)
    push_loops(wide1, 9)

    settle(loop1, loops - 1, recv.at[4])
    joint = fold([loop1[l] for l in range(loops)])
    image_star = joint + RIDGE * g_star
    settle(wide1, loops - 1, recv.at[9])
    sum_mine = in_lines(fold([wide1[l] for l in range(loops)]))
    settle(halo1, 2 * loops, recv.at[5])
    over = fold([halo1[l] for l in range(loops)])
    under = fold([halo1[loops + l] for l in range(loops)])
    ext[4, inner] = sum_mine
    ext[4, 1:2] = over[1:2]
    ext[4, 2 + ROWS_DEV : 3 + ROWS_DEV] = under[0:1]
    row = lax.broadcasted_iota(jnp.int32, (2 + ROWS_DEV, FC), 0)
    inside = ((row > 0) | (tile > 0)) & ((row < 1 + ROWS_DEV) | (tile < tiles - 1))
    image_wide = jnp.where(inside, ext[4, wide] + smooth, 0.0)
    ext[7, wide] = image_wide
    fitted_image = gather_flat(ext[7, inner] / (count_mine + (4.0 * SMOOTH + RIDGE)))
    settle(expo1, tiles - 1, recv.at[3])
    joint = fold([expo1[t] for t in range(tiles)])
    dots0[loop] = joint[EXPO_ROWS:]
    push_loops(dots0, 6)
    image_expo = joint[0:EXPO_ROWS] + RIDGE * g_expo

    def total(buffer, which, size, count):
        settle(buffer, size - 1, recv.at[which])
        joint = fold([buffer[r] for r in range(size)])
        return [
            jnp.sum(jnp.where(quarter == k, joint, 0.0), axis=1, keepdims=True)
            for k in range(count)
        ]

    fitted_image = fitted_image + gather_near(image_star / diag_star, image_expo / diag_expo)
    norm, curve = total(dots0, 6, loops, 2)
    alpha = norm / curve

    res_star = rhs_star - alpha * image_star
    res_expo = rhs_expo - alpha * image_expo
    res_wide = ext[0, wide] - alpha * image_wide
    h_star = res_star / diag_star
    h_expo = res_expo / diag_expo
    ext[5, wide] = res_wide / (ext[1, wide] + (4.0 * SMOOTH + RIDGE))
    ext[6, wide] = res_wide
    h_flat = ext[5, inner]
    fitted = fitted - alpha * fitted_image
    beside = ext[5, 1 : 1 + ROWS_DEV] + ext[5, 3 : 3 + ROWS_DEV] + beside_columns(h_flat)
    dots1[rank] = pack(
        inner_rows(res_star * h_star, res_expo * h_expo, ext[6, inner] * h_flat),
        inner_rows(image_star * h_star, image_expo * h_expo, ext[7, inner] * h_flat),
        lane_fold(weights * fitted * fitted) + inner_rows(
            RIDGE * h_star * h_star,
            RIDGE * h_expo * h_expo,
            (SMOOTH * (4.0 * h_flat - beside) + RIDGE * h_flat) * h_flat,
        ),
    )
    push_dots(dots1, 7)
    norm_next, cross, curve_next = total(dots1, 7, everyone, 3)
    ratio = norm_next / norm
    step = norm_next / (curve_next + ratio * (2.0 * cross + ratio * curve))

    def solve(first, second):
        return alpha * first + step * (second + ratio * first)

    star = solve(g_star, h_star)
    star_out[...] = fold([
        jnp.where(loop == l, star[l * STAR_ROWS : (l + 1) * STAR_ROWS], 0.0) for l in range(loops)
    ])
    expo_out[...] = solve(g_expo, h_expo)
    flat_out[...] = solve(g_flat, h_flat)

    for which, (buffer, count) in enumerate((
        (expo0, tiles - 1), (loop0, loops - 1), (halo0, 2 * loops),
        (expo1, tiles - 1), (loop1, loops - 1), (halo1, 2 * loops),
        (dots0, loops - 1), (dots1, everyone - 1), (wide0, loops - 1), (wide1, loops - 1),
    )):
        settle(buffer, count, send.at[which])


def write_kernel(star, expo, flat, star_out, expo_out, flat_out, sems):
    copies = [
        pltpu.make_async_copy(src, dst, sems.at[k])
        for k, (src, dst) in enumerate(((star, star_out), (expo, expo_out), (flat, flat_out)))
    ]
    for copy in copies:
        copy.start()
    for copy in copies:
        copy.wait()


def on_device(tiles, loops, star_slot, star_block, exposure, superpixel, magnitude, weight):
    blocks = star_slot.shape[1]
    seen = blocks * LANES
    star_wide = loops * STAR_ROWS
    rows = 2 * star_wide + 2 * EXPO_ROWS + FLAT_ROWS
    vmem = pl.BlockSpec(memory_space=pltpu.VMEM)
    hbm = pl.BlockSpec(memory_space=pltpu.HBM)
    out_shape = (
        jax.ShapeDtypeStruct((STAR_ROWS, LANES), F32),
        jax.ShapeDtypeStruct((EXPO_ROWS, LANES), F32),
        jax.ShapeDtypeStruct((ROWS_DEV, FC), F32),
    )
    parts = pl.pallas_call(
        functools.partial(kernel, tiles, loops),
        out_shape=tuple(pltpu.VMEM(x.shape, x.dtype) for x in out_shape),
        in_specs=[hbm] * 6,
        out_specs=(vmem, vmem, vmem),
        scratch_shapes=[
            pltpu.VMEM(star_slot.shape, jnp.int32),
            pltpu.SMEM(star_block.shape, jnp.int32),
            pltpu.VMEM(exposure.shape, jnp.int32),
            pltpu.VMEM(superpixel.shape, jnp.int32),
            pltpu.VMEM(magnitude.shape, F32),
            pltpu.VMEM(weight.shape, F32),
            pltpu.SemaphoreType.DMA((6,)),
            pltpu.VMEM((2 * LANES, seen), BF16),
            pltpu.VMEM((rows, seen), F32),
            pltpu.VMEM((8, FC), F32),
            pltpu.VMEM((2, FC), F32),
            pltpu.VMEM((8, ROWS_DEV + 8, FC), F32),
            pltpu.VMEM((loops, 2 * star_wide, LANES), F32),
            pltpu.VMEM((loops, star_wide, LANES), F32),
            pltpu.VMEM((loops, 2 * FLAT_ROWS, LANES), F32),
            pltpu.VMEM((loops, FLAT_ROWS, LANES), F32),
            pltpu.VMEM((tiles, 2 * EXPO_ROWS, LANES), F32),
            pltpu.VMEM((tiles, EXPO_ROWS + 1, LANES), F32),
            pltpu.VMEM((2 * loops, 8, FC), F32),
            pltpu.VMEM((2 * loops, 2, FC), F32),
            pltpu.VMEM((loops, 1, LANES), F32),
            pltpu.VMEM((tiles * loops, 1, LANES), F32),
            pltpu.SemaphoreType.DMA((10,)),
            pltpu.SemaphoreType.DMA((10,)),
        ],
        compiler_params=pltpu.CompilerParams(
            collective_id=0, has_side_effects=True, vmem_limit_bytes=32 * 1024 * 1024
        ),
    )(*[
        pltpu.with_memory_space_constraint(x, pltpu.HBM)
        for x in (star_slot, star_block, exposure, superpixel, magnitude, weight)
    ])
    star, expo, flat = pl.pallas_call(
        write_kernel,
        out_shape=out_shape,
        in_specs=[vmem] * 3,
        out_specs=(hbm,) * 3,
        scratch_shapes=[pltpu.SemaphoreType.DMA((3,))],
        compiler_params=pltpu.CompilerParams(vmem_limit_bytes=1024 * 1024),
    )(*parts)
    return star.reshape(-1), expo.reshape(-1), flat


def solution(mesh):
    in_specs = (
        P("tile", "loop", None),
        P("tile", "loop"),
        P("tile", "loop", None),
        P("tile", "loop", None),
        P("tile", "loop", None),
        P("tile", "loop", None),
    )
    out_specs = (P(("tile", "loop")), P("loop"), P("tile", None))
    return jax.shard_map(
        functools.partial(on_device, mesh.shape["tile"], mesh.shape["loop"]),
        mesh=mesh, in_specs=in_specs, out_specs=out_specs, check_vma=False,
    )
```

```python
import functools

import jax
import jax.numpy as jnp
from jax import lax
from jax.experimental import pallas as pl
from jax.experimental.pallas import tpu as pltpu
from jax.sharding import PartitionSpec as P

FC = 256
ROWS_DEV = 8
SBLK_DEV = 2
EXP_DEV = 512
STAR_BLK = 256

SMOOTH = 2.0
RIDGE = 0.5

LANES = 128
HALF = LANES // 2
HALVES = FC // LANES
STAR_ROWS = SBLK_DEV * STAR_BLK // LANES
EXPO_ROWS = EXP_DEV // LANES
FLAT_ROWS = HALVES * ROWS_DEV
MESH = pl.DeviceIdType.MESH
F32 = jnp.float32
BF16 = jnp.bfloat16


def pieces(values):
    high = values.astype(BF16).astype(F32)
    return high, values - high


def fold(items):
    total = items[0]
    for item in items[1:]:
        total = total + item
    return total


def lane_fold(row):
    row = jnp.sum(row, axis=0, keepdims=True)
    return fold([row[:, at : at + LANES] for at in range(0, row.shape[1], LANES)])


def line(rows):
    return jnp.concatenate([rows[b : b + 1, :] for b in range(rows.shape[0])], axis=1)


def beside_columns(flat):
    column = lax.broadcasted_iota(jnp.int32, flat.shape, 1)
    left = jnp.where(column == 0, 0.0, pltpu.roll(flat, 1, 1))
    right = jnp.where(column == FC - 1, 0.0, pltpu.roll(flat, FC - 1, 1))
    return left + right


def kernel(
    tiles, loops,
    slot_in, block_in, expo_in, pixel_in, mag_in, weight_in,
    star_out, expo_out, flat_out,
    slot_ref, block_ref, expo_ref, pixel_ref, mag_ref, weight_ref, load,
    hot, mask, edges0, edges1, ext,
    loop0, loop1, wide0, wide1, expo0, expo1, halo0, halo1, dots0, dots1,
    send, recv,
):
    tile = lax.axis_index("tile")
    loop = lax.axis_index("loop")
    everyone = tiles * loops
    rank = tile * loops + loop
    blocks = slot_ref.shape[1]
    per_shard = blocks // loops
    star_wide = loops * STAR_ROWS
    star_rows = 2 * star_wide
    expo_at = star_rows
    flat_at = star_rows + 2 * EXPO_ROWS
    rows = flat_at + FLAT_ROWS

    loads = [
        pltpu.make_async_copy(src, dst, load.at[k])
        for k, (src, dst) in enumerate((
            (slot_in, slot_ref), (block_in, block_ref), (expo_in, expo_ref),
            (pixel_in, pixel_ref), (weight_in, weight_ref), (mag_in, mag_ref),
        ))
    ]
    for copy in loads:
        copy.start()

    def turn(index, d, size):
        index = index + d
        return jnp.where(index >= size, index - size, index)

    def span(first, last, act):
        if last <= 16:
            for d in range(first, last):
                act(d)
            return

        def step(d, carry):
            act(d)
            return carry

        lax.fori_loop(first, last, step, 0)

    def each_other(act):
        for k in range(loops):
            to = turn(loop, k, loops)

            span(0 if k else 1, tiles, lambda d, to=to: act((turn(tile, d, tiles), to)))

    barrier = pltpu.get_barrier_semaphore()
    each_other(
        lambda device: pl.semaphore_signal(barrier, inc=1, device_id=device, device_id_type=MESH)
    )

    def push(src, dst, which, device):
        pltpu.make_async_remote_copy(
            src_ref=src, dst_ref=dst, send_sem=send.at[which], recv_sem=recv.at[which],
            device_id=device, device_id_type=MESH,
        ).start()

    def settle(buffer, count, sem):
        part = buffer.at[pl.ds(0, count)]
        pltpu.make_async_copy(part, part, sem).wait()

    def push_tiles(buffer, which):
        span(1, tiles, lambda d: push(
            buffer.at[tile], buffer.at[tile], which, (turn(tile, d, tiles), loop)
        ))

    def push_loops(buffer, which):
        for d in range(1, loops):
            push(buffer.at[loop], buffer.at[loop], which, (tile, turn(loop, d, loops)))

    def push_edges(edges, buffer, which):
        above = turn(tile, tiles - 1, tiles)
        below = turn(tile, 1, tiles)
        for d in range(loops):
            to = turn(loop, d, loops)
            push(edges, buffer.at[loops + loop], which, (above, to))
            push(edges, buffer.at[loop], which, (below, to))

    def push_dots(buffer, which):
        each_other(lambda device: push(buffer.at[rank], buffer.at[rank], which, device))

    half_ids = lax.broadcasted_iota(jnp.int32, (HALF, LANES), 0)
    lane_ids = lax.broadcasted_iota(jnp.int32, (LANES, LANES), 0)
    star_ids = lax.broadcasted_iota(jnp.int32, (star_rows, LANES), 0)
    expo_ids = lax.broadcasted_iota(jnp.int32, (2 * EXPO_ROWS, LANES), 0)
    flat_ids = lax.broadcasted_iota(jnp.int32, (FLAT_ROWS, LANES), 0)
    for copy in loads:
        copy.wait()
    for b in range(blocks):
        at = slice(b * LANES, (b + 1) * LANES)
        star = block_ref[0, b] * STAR_BLK + slot_ref[0, b : b + 1, :]
        expo = expo_ref[0, b : b + 1, :]
        pixel = pixel_ref[0, b : b + 1, :]
        hot[0:HALF, at] = jnp.where(half_ids == (star & (HALF - 1)), 1.0, 0.0).astype(BF16)
        hot[HALF:LANES, at] = jnp.where(half_ids == (expo & (HALF - 1)), 1.0, 0.0).astype(BF16)
        hot[LANES : 2 * LANES, at] = jnp.where(lane_ids == (pixel & (LANES - 1)), 1.0, 0.0).astype(BF16)
        star_high = (
            (b // per_shard) * (2 * STAR_ROWS) + ((star // HALF) & 1) * STAR_ROWS + star // LANES
        )
        expo_high = ((expo // HALF) & 1) * EXPO_ROWS + expo // LANES
        pixel_high = (pixel // LANES) % HALVES * ROWS_DEV + pixel // FC
        mask[0:star_rows, at] = jnp.where(star_ids == star_high, 1.0, 0.0)
        mask[expo_at:flat_at, at] = jnp.where(expo_ids == expo_high, 1.0, 0.0)
        mask[flat_at:rows, at] = jnp.where(flat_ids == pixel_high, 1.0, 0.0)

    weights = line(weight_ref[0])
    weighted = weights * line(mag_ref[0])

    def lower(count):
        return lax.broadcasted_iota(jnp.int32, (count, LANES), 1) < HALF

    def swap(part):
        return pltpu.roll(part, HALF, 1)

    def spread(values, mine, columns):
        parts = jnp.concatenate(
            [mask[mine] * piece for value in values for piece in pieces(value)], axis=0
        )
        sums = lax.dot_general(
            parts.astype(BF16), hot[columns], (((1,), (1,)), ((), ())), preferred_element_type=F32
        )
        size = mine.stop - mine.start
        return [
            sums[2 * k * size : (2 * k + 1) * size] + sums[(2 * k + 1) * size : (2 * k + 2) * size]
            for k in range(len(values))
        ]

    near = slice(0, flat_at)
    far = slice(flat_at, rows)
    near_columns = slice(0, LANES)
    far_columns = slice(LANES, 2 * LANES)

    def scatter_near(*values):
        out = []
        for left in spread(values, near, near_columns):
            star = []
            for at in range(0, star_rows, 2 * STAR_ROWS):
                low = left[at : at + STAR_ROWS]
                high = left[at + STAR_ROWS : at + 2 * STAR_ROWS]
                star.append(jnp.where(lower(STAR_ROWS), low, swap(high)))
            low, high = left[expo_at : expo_at + EXPO_ROWS], left[expo_at + EXPO_ROWS : flat_at]
            out.append((
                jnp.concatenate(star, axis=0), jnp.where(lower(EXPO_ROWS), swap(low), high)
            ))
        return out

    def scatter_flat(*values):
        return spread(values, far, far_columns)

    def in_lines(flat):
        return jnp.concatenate(
            [flat[h * ROWS_DEV : (h + 1) * ROWS_DEV] for h in range(HALVES)], axis=1
        )

    def find(values, mine, columns):
        size = mine.stop - mine.start
        found = jnp.dot(
            jnp.concatenate(pieces(values), axis=0).astype(BF16), hot[columns],
            preferred_element_type=F32,
        )
        return jnp.sum((found[0:size] + found[size:]) * mask[mine], axis=0, keepdims=True)

    def gather_near(star, expo):
        parts = []
        for at in range(0, star_wide, STAR_ROWS):
            part = star[at : at + STAR_ROWS]
            parts += [part, swap(part)]
        star = jnp.where(lower(star_rows), jnp.concatenate(parts, axis=0), 0.0)
        expo = jnp.where(lower(2 * EXPO_ROWS), 0.0, jnp.concatenate([swap(expo), expo], axis=0))
        return find(jnp.concatenate([star, expo], axis=0), near, near_columns)

    def gather_flat(flat):
        halves = [flat[:, h * LANES : (h + 1) * LANES] for h in range(HALVES)]
        return find(jnp.concatenate(halves, axis=0), far, far_columns)

    quarter = lax.broadcasted_iota(jnp.int32, (1, LANES), 1) // (LANES // 4)

    def pack(*parts):
        both = jnp.concatenate(parts, axis=0)
        both = both + pltpu.roll(both, HALF, 1)
        both = both + pltpu.roll(both, HALF // 2, 1)
        row = both[0:1]
        for k in range(1, len(parts)):
            row = jnp.where(quarter == k, both[k : k + 1], row)
        return row

    (rhs, count) = scatter_near(weighted, weights)
    expo0[tile] = jnp.concatenate([rhs[1], count[1]], axis=0)
    loop0[loop] = jnp.concatenate([rhs[0], count[0]], axis=0)
    pl.semaphore_wait(barrier, everyone - 1)
    push_tiles(expo0, 0)
    push_loops(loop0, 1)
    (rhs, count) = scatter_flat(weighted, weights)
    wide0[loop] = jnp.concatenate([rhs, count], axis=0)
    rhs, count = in_lines(rhs), in_lines(count)
    edges0[0:2] = rhs[0:2]
    edges0[2:4] = count[0:2]
    edges0[4:6] = rhs[ROWS_DEV - 2 :]
    edges0[6:8] = count[ROWS_DEV - 2 :]
    push_edges(edges0, halo0, 2)
    push_loops(wide0, 8)

    settle(loop0, loops - 1, recv.at[1])
    joint = fold([loop0[l] for l in range(loops)])
    rhs_star = joint[0:star_wide]
    diag_star = joint[star_wide : 2 * star_wide] + RIDGE
    settle(wide0, loops - 1, recv.at[8])
    joint = fold([wide0[l] for l in range(loops)])
    rhs_mine = in_lines(joint[0:FLAT_ROWS])
    count_mine = in_lines(joint[FLAT_ROWS:])
    settle(halo0, 2 * loops, recv.at[2])
    over = fold([halo0[l] for l in range(loops)])
    under = fold([halo0[loops + l] for l in range(loops)])
    over = jnp.where(tile > 0, over, 0.0)
    under = jnp.where(tile < tiles - 1, under, 0.0)
    inner = slice(2, 2 + ROWS_DEV)
    wide = slice(1, 3 + ROWS_DEV)
    whole = slice(0, 4 + ROWS_DEV)
    ext[0, inner] = rhs_mine
    ext[0, 0:2] = over[4:6]
    ext[0, 2 + ROWS_DEV : 4 + ROWS_DEV] = under[0:2]
    ext[1, inner] = count_mine
    ext[1, 0:2] = over[6:8]
    ext[1, 2 + ROWS_DEV : 4 + ROWS_DEV] = under[2:4]
    ext[2, whole] = ext[0, whole] / (ext[1, whole] + (4.0 * SMOOTH + RIDGE))
    g_star = rhs_star / diag_star
    g_flat = ext[2, inner]
    fitted = gather_flat(g_flat)
    settle(expo0, tiles - 1, recv.at[0])
    joint = fold([expo0[t] for t in range(tiles)])
    rhs_expo = joint[0:EXPO_ROWS]
    diag_expo = joint[EXPO_ROWS:] + RIDGE
    g_expo = rhs_expo / diag_expo

    shard_row = lax.broadcasted_iota(jnp.int32, (star_wide, LANES), 0) // STAR_ROWS
    own_star = jnp.where(shard_row == loop, 1.0, 0.0)
    own_expo = jnp.where(tile == 0, 1.0, 0.0)
    own_flat = jnp.where(loop == 0, 1.0, 0.0)

    def inner_rows(star, expo, flat):
        return (
            lane_fold(own_star * star) + own_expo * lane_fold(expo) + own_flat * lane_fold(flat)
        )

    fitted = fitted + gather_near(g_star, g_expo)
    pulled = weights * fitted
    ((sum_star, sum_expo),) = scatter_near(pulled)
    expo1[tile] = sum_expo
    loop1[loop] = sum_star
    push_tiles(expo1, 3)
    push_loops(loop1, 4)
    (sum_flat,) = scatter_flat(pulled)
    wide1[loop] = sum_flat
    sum_flat = in_lines(sum_flat)
    edges1[0:1] = sum_flat[0:1]
    edges1[1:2] = sum_flat[ROWS_DEV - 1 :]
    push_edges(edges1, halo1, 5)
    push_loops(wide1, 9)
    v = ext[2, wide]
    smooth = SMOOTH * (4.0 * v - ext[2, 0 : 2 + ROWS_DEV] - ext[2, 2 : 4 + ROWS_DEV] - beside_columns(v)) + RIDGE * v
    ext[3, wide] = smooth
    smooth_mine = ext[3, inner]
    dots0[rank] = pack(
        inner_rows(rhs_star * g_star, rhs_expo * g_expo, rhs_mine * g_flat),
        lane_fold(pulled * fitted) + inner_rows(
            RIDGE * g_star * g_star, RIDGE * g_expo * g_expo, smooth_mine * g_flat
        ),
    )
    push_dots(dots0, 6)

    settle(loop1, loops - 1, recv.at[4])
    joint = fold([loop1[l] for l in range(loops)])
    image_star = joint + RIDGE * g_star
    settle(wide1, loops - 1, recv.at[9])
    sum_mine = in_lines(fold([wide1[l] for l in range(loops)]))
    settle(halo1, 2 * loops, recv.at[5])
    over = fold([halo1[l] for l in range(loops)])
    under = fold([halo1[loops + l] for l in range(loops)])
    ext[4, inner] = sum_mine
    ext[4, 1:2] = over[1:2]
    ext[4, 2 + ROWS_DEV : 3 + ROWS_DEV] = under[0:1]
    row = lax.broadcasted_iota(jnp.int32, (2 + ROWS_DEV, FC), 0)
    inside = ((row > 0) | (tile > 0)) & ((row < 1 + ROWS_DEV) | (tile < tiles - 1))
    image_wide = jnp.where(inside, ext[4, wide] + smooth, 0.0)
    ext[7, wide] = image_wide
    fitted_image = gather_flat(ext[7, inner] / (count_mine + (4.0 * SMOOTH + RIDGE)))
    settle(expo1, tiles - 1, recv.at[3])
    joint = fold([expo1[t] for t in range(tiles)])
    image_expo = joint + RIDGE * g_expo

    def total(buffer, which, count):
        settle(buffer, everyone - 1, recv.at[which])
        joint = fold([buffer[r] for r in range(everyone)])
        return [
            jnp.sum(jnp.where(quarter == k, joint, 0.0), axis=1, keepdims=True)
            for k in range(count)
        ]

    fitted_image = fitted_image + gather_near(image_star / diag_star, image_expo / diag_expo)
    norm, curve = total(dots0, 6, 2)
    alpha = norm / curve

    res_star = rhs_star - alpha * image_star
    res_expo = rhs_expo - alpha * image_expo
    res_wide = ext[0, wide] - alpha * image_wide
    h_star = res_star / diag_star
    h_expo = res_expo / diag_expo
    ext[5, wide] = res_wide / (ext[1, wide] + (4.0 * SMOOTH + RIDGE))
    ext[6, wide] = res_wide
    h_flat = ext[5, inner]
    fitted = fitted - alpha * fitted_image
    beside = ext[5, 1 : 1 + ROWS_DEV] + ext[5, 3 : 3 + ROWS_DEV] + beside_columns(h_flat)
    dots1[rank] = pack(
        inner_rows(res_star * h_star, res_expo * h_expo, ext[6, inner] * h_flat),
        inner_rows(image_star * h_star, image_expo * h_expo, ext[7, inner] * h_flat),
        lane_fold(weights * fitted * fitted) + inner_rows(
            RIDGE * h_star * h_star,
            RIDGE * h_expo * h_expo,
            (SMOOTH * (4.0 * h_flat - beside) + RIDGE * h_flat) * h_flat,
        ),
    )
    push_dots(dots1, 7)
    norm_next, cross, curve_next = total(dots1, 7, 3)
    ratio = norm_next / norm
    step = norm_next / (curve_next + ratio * (2.0 * cross + ratio * curve))

    def solve(first, second):
        return alpha * first + step * (second + ratio * first)

    star = solve(g_star, h_star)
    star_out[...] = fold([
        jnp.where(loop == l, star[l * STAR_ROWS : (l + 1) * STAR_ROWS], 0.0) for l in range(loops)
    ])
    expo_out[...] = solve(g_expo, h_expo)
    flat_out[...] = solve(g_flat, h_flat)

    for which, (buffer, count) in enumerate((
        (expo0, tiles - 1), (loop0, loops - 1), (halo0, 2 * loops),
        (expo1, tiles - 1), (loop1, loops - 1), (halo1, 2 * loops),
        (dots0, everyone - 1), (dots1, everyone - 1), (wide0, loops - 1), (wide1, loops - 1),
    )):
        settle(buffer, count, send.at[which])


def write_kernel(star, expo, flat, star_out, expo_out, flat_out, sems):
    copies = [
        pltpu.make_async_copy(src, dst, sems.at[k])
        for k, (src, dst) in enumerate(((star, star_out), (expo, expo_out), (flat, flat_out)))
    ]
    for copy in copies:
        copy.start()
    for copy in copies:
        copy.wait()


def on_device(tiles, loops, star_slot, star_block, exposure, superpixel, magnitude, weight):
    blocks = star_slot.shape[1]
    seen = blocks * LANES
    star_wide = loops * STAR_ROWS
    rows = 2 * star_wide + 2 * EXPO_ROWS + FLAT_ROWS
    vmem = pl.BlockSpec(memory_space=pltpu.VMEM)
    hbm = pl.BlockSpec(memory_space=pltpu.HBM)
    out_shape = (
        jax.ShapeDtypeStruct((STAR_ROWS, LANES), F32),
        jax.ShapeDtypeStruct((EXPO_ROWS, LANES), F32),
        jax.ShapeDtypeStruct((ROWS_DEV, FC), F32),
    )
    parts = pl.pallas_call(
        functools.partial(kernel, tiles, loops),
        out_shape=tuple(pltpu.VMEM(x.shape, x.dtype) for x in out_shape),
        in_specs=[hbm] * 6,
        out_specs=(vmem, vmem, vmem),
        scratch_shapes=[
            pltpu.VMEM(star_slot.shape, jnp.int32),
            pltpu.SMEM(star_block.shape, jnp.int32),
            pltpu.VMEM(exposure.shape, jnp.int32),
            pltpu.VMEM(superpixel.shape, jnp.int32),
            pltpu.VMEM(magnitude.shape, F32),
            pltpu.VMEM(weight.shape, F32),
            pltpu.SemaphoreType.DMA((6,)),
            pltpu.VMEM((2 * LANES, seen), BF16),
            pltpu.VMEM((rows, seen), F32),
            pltpu.VMEM((8, FC), F32),
            pltpu.VMEM((2, FC), F32),
            pltpu.VMEM((8, ROWS_DEV + 8, FC), F32),
            pltpu.VMEM((loops, 2 * star_wide, LANES), F32),
            pltpu.VMEM((loops, star_wide, LANES), F32),
            pltpu.VMEM((loops, 2 * FLAT_ROWS, LANES), F32),
            pltpu.VMEM((loops, FLAT_ROWS, LANES), F32),
            pltpu.VMEM((tiles, 2 * EXPO_ROWS, LANES), F32),
            pltpu.VMEM((tiles, EXPO_ROWS, LANES), F32),
            pltpu.VMEM((2 * loops, 8, FC), F32),
            pltpu.VMEM((2 * loops, 2, FC), F32),
            pltpu.VMEM((tiles * loops, 1, LANES), F32),
            pltpu.VMEM((tiles * loops, 1, LANES), F32),
            pltpu.SemaphoreType.DMA((10,)),
            pltpu.SemaphoreType.DMA((10,)),
        ],
        compiler_params=pltpu.CompilerParams(
            collective_id=0, has_side_effects=True, vmem_limit_bytes=32 * 1024 * 1024
        ),
    )(*[
        pltpu.with_memory_space_constraint(x, pltpu.HBM)
        for x in (star_slot, star_block, exposure, superpixel, magnitude, weight)
    ])
    star, expo, flat = pl.pallas_call(
        write_kernel,
        out_shape=out_shape,
        in_specs=[vmem] * 3,
        out_specs=(hbm,) * 3,
        scratch_shapes=[pltpu.SemaphoreType.DMA((3,))],
        compiler_params=pltpu.CompilerParams(vmem_limit_bytes=1024 * 1024),
    )(*parts)
    return star.reshape(-1), expo.reshape(-1), flat


def solution(mesh):
    in_specs = (
        P("tile", "loop", None),
        P("tile", "loop"),
        P("tile", "loop", None),
        P("tile", "loop", None),
        P("tile", "loop", None),
        P("tile", "loop", None),
    )
    out_specs = (P(("tile", "loop")), P("loop"), P("tile", None))
    return jax.shard_map(
        functools.partial(on_device, mesh.shape["tile"], mesh.shape["loop"]),
        mesh=mesh, in_specs=in_specs, out_specs=out_specs, check_vma=False,
    )
```
